32 devices in a mesh: grp: 4 (over z), srv: 8 (over y, x, core).
Axes of the slice: x: 2, y: 2, z: 4, core: 2. Of those that a mesh axis runs over, the one named last changes fastest.
Arguments:
- queries: bfloat16 [2048, 1024], P('srv', 'grp'), may hold values from -8 to 8
- key_rows: bfloat16 [2048, 128], P('srv'), may hold values from -8 to 8
- value_rows: bfloat16 [2048, 128], P('srv'), may hold values from -6 to 6
- grad_output: bfloat16 [2048, 1024], P('srv', 'grp'), may hold values from -6 to 6
- doc_ids: int32 [2048], replicated, may hold values from 0 to 7, never falling along the last dimension, each value on 1 to 1280 neighbouring positions
Outputs:
- grad_query: bfloat16 [2048, 1024], P('srv', 'grp')
- grad_key: bfloat16 [2048, 128], P('srv', 'grp')
- grad_value: bfloat16 [2048, 128], P('srv', 'grp')
The draws below stay inside these ranges and needn't reach their ends.
Inputs may be any that keep to these rules, and one draw needn't show every extreme that they name: `doc_ids`: document numbers never fall along the pack; each document has 1 to 1280 tokens, and one has exactly 1280.
All inputs are finite; a program needn't handle non-finite values.
Results may differ from the reference program's by a relative error of at most 0.0069.
Values may be sent and summed in bfloat16 or wider, within the bound.
No kernel may reach another device: no remote copies, remote signals or barrier semaphores. Data moves between devices by JAX's collectives and lax.ppermute only.
A program may use at most 64 MiB of HBM per device.

```python
import math
import jax
import jax.numpy as jnp
import numpy as np
from jax import lax

HD = 128
H = 8
KVH = 1
TOKENS = 2048
DOC_MOST = 1280
DOC_COUNT = 8


def draw_queries(key, part):
    base = jax.random.normal(jax.random.fold_in(key, 2), (TOKENS, H * HD), jnp.float32)
    return base.astype(jnp.bfloat16)


def draw_key_rows(key, part):
    base = jax.random.normal(jax.random.fold_in(key, 1), (TOKENS, KVH * HD), jnp.float32)
    return base.astype(jnp.bfloat16)


def shard_levels(key, shape, shards, least, high):
    def one(dim, shards_of):
        heights = jax.random.uniform(jax.random.fold_in(jax.random.fold_in(key, 6), dim), (shards_of,), jnp.float32, least / len(shards), high / len(shards))
        return jnp.repeat(jnp.exp(heights), shape[dim] // shards_of).reshape((-1,) + (1,) * (len(shape) - dim - 1))

    level = one(*shards[0])
    for cut in shards[1:]:
        level = level * one(*cut)
    return level


def split_up(count, total, most, skew):
    portions = [(1 << 20) // math.isqrt(grade ** skew) + 1 for grade in range(2, count + 1)]
    spare, holding = total - most - (count - 1), [1] * (count - 1)
    while spare > 0:
        movable = [i for i in range(count - 1) if holding[i] < most]
        pool, left = sum([portions[i] for i in movable]), spare
        for i in movable:
            extra = min(most - holding[i], max(1, left * portions[i] // pool), spare)
            holding[i] = holding[i] + extra
            spare = spare - extra
    return np.array([most] + holding)


def ragged_sizes(stream_key, amount, total, limit, lean):
    if amount == 2:
        one = jax.random.randint(stream_key, (), max(1, total - limit), min(limit, total - 1) + 1)
        return jnp.stack([one, total - one])
    lengths = jnp.asarray(split_up(amount, total, limit, lean), jnp.int32)
    pairs = (amount - 1) // 2
    donor, receiver = lengths[1:1 + 2 * pairs:2], lengths[2:2 + 2 * pairs:2]
    margin = jnp.minimum(donor - 1, limit - receiver)
    shifted = jax.random.randint(jax.random.fold_in(stream_key, 1), (pairs,), 0, 1 << 20) % (margin + 1)
    lengths = lengths.at[1:1 + 2 * pairs:2].set(donor - shifted).at[2:2 + 2 * pairs:2].set(receiver + shifted)
    return lengths[jax.random.permutation(jax.random.fold_in(stream_key, 2), amount)]


def noise(own_key, extent, spread, reach, cuts=(), kind=jnp.bfloat16):
    values = spread * jax.random.normal(own_key, extent, jnp.float32)
    if cuts:
        values = values * shard_levels(own_key, extent, cuts, -0.22, 0.18)
    return jnp.clip(values, -reach, reach).astype(kind)


def setup_inputs(seed: int = 0) -> dict:
    splits = jax.random.split(jax.random.key(seed), 6)
    return {
        "queries": draw_queries(jax.random.fold_in(splits[5], 71), 0),
        "key_rows": draw_key_rows(jax.random.fold_in(splits[5], 71), 0),
        "value_rows": noise(splits[2], (TOKENS, KVH * HD), 1.0, 6.0, ((0, 8),)),
        "grad_output": noise(splits[3], (TOKENS, H * HD), 1.0, 6.0, ((0, 8), (1, 4))),
        "doc_ids": jnp.searchsorted(jnp.cumsum(ragged_sizes(splits[4], DOC_COUNT, TOKENS, DOC_MOST, 2)), jnp.arange(TOKENS), side="right").astype(jnp.int32),
    }


big_negative = -1.0e30


def reference(queries, key_rows, value_rows, grad_output, doc_ids):
    score_scale = HD ** -0.5
    ratio = H // KVH
    positions = jnp.arange(TOKENS, dtype=jnp.int32)
    allowed = (doc_ids[:, None] == doc_ids[None, :]) & (positions[None, :] <= positions[:, None])

    def one_head(head_index):
        kv_index = head_index // ratio
        query_head = lax.dynamic_slice_in_dim(queries, head_index * HD, HD, 1)
        grad_head = lax.dynamic_slice_in_dim(grad_output, head_index * HD, HD, 1)
        key_head = lax.dynamic_slice_in_dim(key_rows, kv_index * HD, HD, 1)
        value_head = lax.dynamic_slice_in_dim(value_rows, kv_index * HD, HD, 1)
        scores = jnp.dot(query_head, key_head.T, preferred_element_type=jnp.float32) * score_scale
        masked = jnp.where(allowed, scores, big_negative)
        row_max = jnp.max(masked, axis=1, keepdims=True)
        row_sum = jnp.sum(jnp.where(allowed, jnp.exp(masked - row_max), 0.0), axis=1, keepdims=True)
        log_norm = row_max + jnp.log(row_sum)
        weights = jnp.where(allowed, jnp.exp(scores - log_norm), 0.0)
        grad_probs = jnp.dot(grad_head, value_head.T, preferred_element_type=jnp.float32)
        row_delta = jnp.sum(weights * grad_probs, axis=1, keepdims=True)
        grad_scores = (weights * (grad_probs - row_delta)).astype(jnp.bfloat16)
        weights_low = weights.astype(jnp.bfloat16)
        grad_query = (jnp.dot(grad_scores, key_head, preferred_element_type=jnp.float32) * score_scale).astype(jnp.bfloat16)
        grad_key = jnp.dot(grad_scores.T, query_head, preferred_element_type=jnp.float32) * score_scale
        grad_value = jnp.dot(weights_low.T, grad_head, preferred_element_type=jnp.float32)
        return grad_query, grad_key, grad_value

    grad_query, grad_key, grad_value = lax.map(one_head, jnp.arange(H, dtype=jnp.int32))
    grad_query = grad_query.transpose(1, 0, 2).reshape(TOKENS, H * HD)
    grad_key = grad_key.reshape(KVH, ratio, TOKENS, HD).sum(axis=1)
    grad_value = grad_value.reshape(KVH, ratio, TOKENS, HD).sum(axis=1)
    grad_key = grad_key.transpose(1, 0, 2).reshape(TOKENS, KVH * HD).astype(jnp.bfloat16)
    grad_value = grad_value.transpose(1, 0, 2).reshape(TOKENS, KVH * HD).astype(jnp.bfloat16)
    return (grad_query, grad_key, grad_value)
```

```python
import functools

import jax
import jax.numpy as jnp
from jax import lax
from jax.experimental import pallas as pl
from jax.experimental.pallas import tpu as pltpu
from jax.sharding import PartitionSpec as P

HD = 128
SCALE = HD**-0.5
LOG2E = 1.4426950408889634
MASKED = -1.0e30
LOWEST = -1.0e20
F32 = jnp.float32
BF16 = jnp.bfloat16


def nn(a, b):
    return lax.dot_general(a, b, (((1,), (0,)), ((), ())), preferred_element_type=F32)


def nt(a, b):
    return lax.dot_general(a, b, (((1,), (1,)), ((), ())), preferred_element_type=F32)


def tn(a, b):
    return lax.dot_general(a, b, (((0,), (0,)), ((), ())), preferred_element_type=F32)


def key_doc_column(docs_ref, block):
    row = docs_ref[pl.ds(block, 1), :]
    span = row.shape[1]
    column = jnp.transpose(jnp.broadcast_to(row, (128, span)))
    return jnp.concatenate([column] * (span // 128), axis=1)


def scores_of(kv, qt, key_doc, row_doc, causal):
    scores = nn(kv[:, :HD], qt) * (SCALE * LOG2E)
    allowed = key_doc == row_doc
    if causal:
        key_pos = lax.broadcasted_iota(jnp.int32, scores.shape, 0)
        row_pos = lax.broadcasted_iota(jnp.int32, scores.shape, 1)
        allowed = allowed & (key_pos <= row_pos)
    return jnp.where(allowed, scores, MASKED)


def add_stats(stats_ref, kv, qt_ref, dot_ref, docs_ref, key_block, row_block, chunks, causal):
    rows = docs_ref.shape[1]
    key_doc = key_doc_column(docs_ref, key_block)
    row_doc = docs_ref[pl.ds(row_block, 1), :]
    for chunk in chunks:
        lanes = slice(chunk * rows, (chunk + 1) * rows)
        scores = scores_of(kv, qt_ref[:, lanes], key_doc, row_doc, causal)
        grad_probs = nn(kv[:, HD:], dot_ref[:, lanes])
        old = stats_ref[0:1, lanes]
        new = jnp.maximum(old, jnp.max(scores, axis=0, keepdims=True))
        factor = jnp.exp2(old - new)
        weights = jnp.exp2(scores - new)
        stats_ref[0:1, lanes] = new
        stats_ref[1:2, lanes] = stats_ref[1:2, lanes] * factor + jnp.sum(
            weights, axis=0, keepdims=True
        )
        stats_ref[2:3, lanes] = stats_ref[2:3, lanes] * factor + jnp.sum(
            weights * grad_probs, axis=0, keepdims=True
        )


def add_grads(
    kv, qt_ref, dot_ref, docs_ref, key_block, row_block, chunks, causal, norm_ref, dqt_ref
):
    rows = docs_ref.shape[1]
    key_doc = key_doc_column(docs_ref, key_block)
    row_doc = docs_ref[pl.ds(row_block, 1), :]
    dkt = jnp.zeros((HD, rows), F32)
    dvt = jnp.zeros((HD, rows), F32)
    for chunk in chunks:
        lanes = slice(chunk * rows, (chunk + 1) * rows)
        qt = qt_ref[:, lanes]
        dot = dot_ref[:, lanes]
        scores = scores_of(kv, qt, key_doc, row_doc, causal)
        weights = jnp.exp2(scores - norm_ref[0:1, lanes])
        grad_probs = nn(kv[:, HD:], dot)
        grad_scores = (weights * (grad_probs - norm_ref[1:2, lanes])).astype(BF16)
        dkt += nt(qt, grad_scores)
        dvt += nt(dot, weights.astype(BF16))
        dqt_ref[:, lanes] += tn(kv[:, :HD], grad_scores)
    return dkt, dvt


def place():
    srv = lax.axis_index("srv")
    return srv // 2, srv % 2


def reaches(ids_ref, rows, key_block, row_block):
    return ids_ref[key_block * rows + rows - 1] >= ids_ref[row_block * rows]


def own_stats_kernel(heads, ids_ref, docs_ref, q_own, q_par, do_own, do_par, kv_ref, qt_ref, dot_ref, stats_ref):
    rows = docs_ref.shape[1]
    chip, core = place()
    for side, (q_ref, do_ref) in enumerate(((q_own, do_own), (q_par, do_par))):
        qt = jnp.transpose(q_ref[...])
        dot = jnp.transpose(do_ref[...])
        for head in range(heads):
            lanes = slice((side * heads + head) * rows, (side * heads + head + 1) * rows)
            qt_ref[:, lanes] = qt[head * HD : (head + 1) * HD, :]
            dot_ref[:, lanes] = dot[head * HD : (head + 1) * HD, :]
    stats_ref[...] = jnp.zeros(stats_ref.shape, F32)
    stats_ref[0:1, :] = jnp.full((1, stats_ref.shape[1]), LOWEST, F32)
    block = chip * 2 + core
    kv = kv_ref[...]
    add_stats(stats_ref, kv, qt_ref, dot_ref, docs_ref, block, block, range(heads), True)
    other = chip * 2 + 1 - core

    @pl.when((core == 0) & reaches(ids_ref, rows, block, other))
    def _():
        add_stats(stats_ref, kv, qt_ref, dot_ref, docs_ref, block, other, range(heads, 2 * heads), False)


def each_remote(groups, ids_ref, rows, body):
    chip, core = place()

    def step(group, slot, away):
        source = chip ^ away
        key_block = source * 2 + core
        for side in range(2):
            row_block = chip * 2 + (core if side == 0 else 1 - core)
            active = (source < chip) & reaches(ids_ref, rows, key_block, row_block)
            pl.when(active)(functools.partial(body, group, slot, key_block, row_block, side))

    first = 1
    for group, amount in enumerate(groups):
        if amount == 1:
            step(group, 0, first)
        else:
            base = first

            @pl.loop(0, amount)
            def _(slot):
                step(group, slot, base + slot)

        first += amount


def far_stats_kernel(heads, groups, ids_ref, docs_ref, qt_ref, dot_ref, stats_in, *rest):
    kv_refs, stats_ref = rest[:-1], rest[-1]
    rows = docs_ref.shape[1]
    stats_ref[...] = stats_in[...]

    def body(group, slot, key_block, row_block, side):
        add_stats(
            stats_ref,
            kv_refs[group][slot],
            qt_ref,
            dot_ref,
            docs_ref,
            key_block,
            row_block,
            range(side * heads, (side + 1) * heads),
            False,
        )

    each_remote(groups, ids_ref, rows, body)


def far_grads_kernel(heads, groups, ids_ref, docs_ref, qt_ref, dot_ref, stats_ref, other_ref, *rest):
    count = len(groups)
    kv_refs, out_refs = rest[:count], rest[count : 2 * count]
    dqt_ref, norm_ref = rest[2 * count :]
    rows = docs_ref.shape[1]
    half = heads * rows
    mine = stats_ref[...]
    other = other_ref[...]
    other = jnp.concatenate([other[:, half:], other[:, :half]], axis=1)
    top = jnp.maximum(mine[0:1], other[0:1])
    mine_by = jnp.exp2(mine[0:1] - top)
    other_by = jnp.exp2(other[0:1] - top)
    total = mine[1:2] * mine_by + other[1:2] * other_by
    norm_ref[...] = jnp.zeros(norm_ref.shape, F32)
    norm_ref[0:1, :] = top + jnp.log2(total)
    norm_ref[1:2, :] = (mine[2:3] * mine_by + other[2:3] * other_by) / total
    dqt_ref[...] = jnp.zeros(dqt_ref.shape, F32)
    for out_ref in out_refs:
        out_ref[...] = jnp.zeros(out_ref.shape, BF16)

    def body(group, slot, key_block, row_block, side):
        kv = kv_refs[group][slot]
        dkt, dvt = add_grads(
            kv,
            qt_ref,
            dot_ref,
            docs_ref,
            key_block,
            row_block,
            range(side * heads, (side + 1) * heads),
            False,
            norm_ref,
            dqt_ref,
        )
        both = jnp.concatenate([dkt * SCALE, dvt], axis=0)
        if side == 1:
            both = both + out_refs[group][slot].astype(F32)
        out_refs[group][slot] = both.astype(BF16)

    each_remote(groups, ids_ref, rows, body)


def own_grads_kernel(heads, ids_ref, docs_ref, qt_ref, dot_ref, norm_ref, kv_ref, dqt_in, dkv_ref, dq_own, dq_par, dqt_ref):
    rows = docs_ref.shape[1]
    chip, core = place()
    block = chip * 2 + core
    other = chip * 2 + 1 - core
    dqt_ref[...] = dqt_in[...]
    kv = kv_ref[...]
    dkt, dvt = add_grads(
        kv, qt_ref, dot_ref, docs_ref, block, block, range(heads), True, norm_ref, dqt_ref
    )
    dkv_ref[...] = jnp.concatenate([dkt * SCALE, dvt], axis=0)

    @pl.when((core == 0) & reaches(ids_ref, rows, block, other))
    def _():
        dkt, dvt = add_grads(
            kv, qt_ref, dot_ref, docs_ref, block, other, range(heads, 2 * heads), False, norm_ref, dqt_ref
        )
        dkv_ref[...] += jnp.concatenate([dkt * SCALE, dvt], axis=0)

    for side, out_ref in enumerate((dq_own, dq_par)):
        parts = [
            dqt_ref[:, (side * heads + head) * rows : (side * heads + head + 1) * rows]
            for head in range(heads)
        ]
        out_ref[...] = jnp.concatenate(parts, axis=0) * SCALE


def combine_kernel(share, count, own_ref, dq_own, dq_far, *rest):
    parts, outs = rest[:count], rest[count:]
    dq_ref, keep_ref, send_refs, sum_ref = outs[0], outs[1], outs[2:-1], outs[-1]
    width = HD // share
    total = own_ref[...]
    for part in parts:
        for slot in range(part.shape[0]):
            total = total + part[slot].astype(F32)
    sum_ref[...] = total
    member = lax.axis_index("grp") % share
    for away, out_ref in enumerate((keep_ref, *send_refs)):
        first = pl.multiple_of((member ^ away) * width, width)
        for half in range(2):
            piece = sum_ref[pl.ds(half * HD + first, width), :]
            out_ref[half * width : (half + 1) * width, :] = piece.astype(out_ref.dtype)
    dq_ref[...] = jnp.transpose(dq_own[...] + dq_far[...]).astype(BF16)


def finish_kernel(keep_ref, *rest):
    parts, (dk_ref, dv_ref) = rest[:-2], rest[-2:]
    total = keep_ref[...]
    for part in parts:
        total = total + part[...].astype(F32)
    width = total.shape[0] // 2
    dk_ref[...] = total[:width].astype(BF16)
    dv_ref[...] = total[width:].astype(BF16)


SMEM = pl.BlockSpec(memory_space=pltpu.SMEM)
VMEM = pl.BlockSpec(memory_space=pltpu.VMEM)


def call(kernel, out_shape, operands, scratch=(), smem=0, cost=None):
    return pl.pallas_call(
        kernel,
        out_shape=out_shape,
        in_specs=[SMEM] * smem + [VMEM] * (len(operands) - smem),
        out_specs=[VMEM] * len(out_shape),
        scratch_shapes=list(scratch),
        cost_estimate=cost,
        compiler_params=pltpu.CompilerParams(vmem_limit_bytes=24 << 20),
    )(*operands)


def sds(shape, dtype):
    return jax.ShapeDtypeStruct(shape, dtype)


def on_device(queries, key_rows, value_rows, grad_output, doc_ids):
    rows, columns = queries.shape
    heads = columns // HD
    srv = lax.axis_size("srv")
    chips = srv // 2
    grp = lax.axis_size("grp")
    kv_heads = key_rows.shape[1] // HD
    share = grp // kv_heads
    lanes = 2 * heads * rows
    if kv_heads > 1:
        first = lax.axis_index("grp") // share * HD
        key_rows = lax.dynamic_slice_in_dim(key_rows, first, HD, 1)
        value_rows = lax.dynamic_slice_in_dim(value_rows, first, HD, 1)
    own_kv = jnp.concatenate([key_rows, value_rows], axis=1)
    docs = doc_ids.reshape(srv, rows)

    def swap(block):
        return lax.ppermute(block, "srv", [(i, i ^ 1) for i in range(srv)])

    up = [
        [(i, i ^ 2 * away) for i in range(srv) if i ^ 2 * away > i] for away in range(chips)
    ]
    far_kv = [lax.ppermute(own_kv, "srv", up[away])[None] for away in range(1, chips)]
    groups = [1] * len(far_kv)
    if chips > 4:
        groups = [len(far_kv)]
        far_kv = [jnp.concatenate(far_kv, axis=0)]
    q_par = swap(queries)
    do_par = swap(grad_output)

    work = 2 * rows * rows * HD * heads
    qt, dot, stats = call(
        functools.partial(own_stats_kernel, heads),
        [sds((HD, lanes), BF16), sds((HD, lanes), BF16), sds((8, lanes), F32)],
        [doc_ids, docs, queries, q_par, grad_output, do_par, own_kv],
        smem=1,
        cost=pl.CostEstimate(flops=work * 4, bytes_accessed=2 << 20, transcendentals=0),
    )
    (stats,) = call(
        functools.partial(far_stats_kernel, heads, groups),
        [sds((8, lanes), F32)],
        [doc_ids, docs, qt, dot, stats, *far_kv],
        smem=1,
    )
    other_stats = swap(stats)
    *far_dkv, dqt, norm = call(
        functools.partial(far_grads_kernel, heads, groups),
        [sds((amount, 2 * HD, rows), BF16) for amount in groups]
        + [sds((HD, lanes), F32), sds((8, lanes), F32)],
        [doc_ids, docs, qt, dot, stats, other_stats, *far_kv],
        smem=1,
    )
    if chips > 4:
        far_dkv = [far_dkv[0][i : i + 1] for i in range(chips - 1)]
    came = [
        lax.ppermute(part, "srv", [(b, a) for a, b in up[away + 1]])
        for away, part in enumerate(far_dkv)
    ]
    own_dkv, dq_own, dq_par = call(
        functools.partial(own_grads_kernel, heads),
        [sds((2 * HD, rows), F32)] + [sds((columns, rows), F32)] * 2,
        [doc_ids, docs, qt, dot, norm, own_kv, dqt],
        scratch=[pltpu.VMEM((HD, lanes), F32)],
        smem=1,
        cost=pl.CostEstimate(flops=work * 6, bytes_accessed=2 << 20, transcendentals=0),
    )
    dq_far = swap(dq_par)
    width = HD // share
    grad_query, keep, *send = call(
        functools.partial(combine_kernel, share, len(came)),
        [sds((rows, columns), BF16), sds((2 * width, rows), F32)]
        + [sds((2 * width, rows), BF16)] * (share - 1),
        [own_dkv, dq_own, dq_far, *came],
        scratch=[pltpu.VMEM((2 * HD, rows), F32)],
    )
    back = [
        lax.ppermute(part, "grp", [(i, i ^ (away + 1)) for i in range(grp)])
        for away, part in enumerate(send)
    ]
    grad_key, grad_value = call(
        finish_kernel, [sds((width, rows), BF16)] * 2, [keep, *back]
    )
    return grad_query, grad_key.T, grad_value.T


def solution(mesh):
    in_specs = (P("srv", "grp"), P("srv", None), P("srv", None), P("srv", "grp"), P())
    out_specs = (P("srv", "grp"), P("srv", "grp"), P("srv", "grp"))
    return jax.shard_map(
        on_device, mesh=mesh, in_specs=in_specs, out_specs=out_specs, check_vma=False
    )
```

```python
import functools

import jax
import jax.numpy as jnp
from jax import lax
from jax.experimental import pallas as pl
from jax.experimental.pallas import tpu as pltpu
from jax.sharding import PartitionSpec as P

HD = 128
SCALE = HD**-0.5
LOG2E = 1.4426950408889634
MASKED = -1.0e30
LOWEST = -1.0e20
F32 = jnp.float32
BF16 = jnp.bfloat16


def nn(a, b):
    return lax.dot_general(a, b, (((1,), (0,)), ((), ())), preferred_element_type=F32)


def nt(a, b):
    return lax.dot_general(a, b, (((1,), (1,)), ((), ())), preferred_element_type=F32)


def tn(a, b):
    return lax.dot_general(a, b, (((0,), (0,)), ((), ())), preferred_element_type=F32)


def key_doc_column(docs_ref, block):
    row = docs_ref[pl.ds(block, 1), :]
    span = row.shape[1]
    column = jnp.transpose(jnp.broadcast_to(row, (128, span)))
    return jnp.concatenate([column] * (span // 128), axis=1)


def scores_of(kv, qt, key_doc, row_doc, causal):
    scores = nn(kv[:, :HD], qt) * (SCALE * LOG2E)
    allowed = key_doc == row_doc
    if causal:
        key_pos = lax.broadcasted_iota(jnp.int32, scores.shape, 0)
        row_pos = lax.broadcasted_iota(jnp.int32, scores.shape, 1)
        allowed = allowed & (key_pos <= row_pos)
    return jnp.where(allowed, scores, MASKED)


def add_stats(stats_ref, kv, qd_ref, docs_ref, key_block, row_block, side, causal):
    rows = docs_ref.shape[1]
    key_doc = key_doc_column(docs_ref, key_block)
    row_doc = docs_ref[pl.ds(row_block, 1), :]
    heads = qd_ref.shape[1] // rows
    for head in range(heads):
        local = slice(head * rows, (head + 1) * rows)
        lanes = slice((side * heads + head) * rows, (side * heads + head + 1) * rows)
        scores = scores_of(kv, qd_ref[:HD, local], key_doc, row_doc, causal)
        grad_probs = nn(kv[:, HD:], qd_ref[HD:, local])
        old = stats_ref[0:1, lanes]
        new = jnp.maximum(old, jnp.max(scores, axis=0, keepdims=True))
        factor = jnp.exp2(old - new)
        weights = jnp.exp2(scores - new)
        stats_ref[0:1, lanes] = new
        stats_ref[1:2, lanes] = stats_ref[1:2, lanes] * factor + jnp.sum(
            weights, axis=0, keepdims=True
        )
        stats_ref[2:3, lanes] = stats_ref[2:3, lanes] * factor + jnp.sum(
            weights * grad_probs, axis=0, keepdims=True
        )


def add_grads(kv, qd_ref, docs_ref, key_block, row_block, side, causal, norm_ref, dqt_ref):
    rows = docs_ref.shape[1]
    key_doc = key_doc_column(docs_ref, key_block)
    row_doc = docs_ref[pl.ds(row_block, 1), :]
    dkt = jnp.zeros((HD, rows), F32)
    dvt = jnp.zeros((HD, rows), F32)
    heads = qd_ref.shape[1] // rows
    for head in range(heads):
        local = slice(head * rows, (head + 1) * rows)
        lanes = slice((side * heads + head) * rows, (side * heads + head + 1) * rows)
        qt = qd_ref[:HD, local]
        dot = qd_ref[HD:, local]
        scores = scores_of(kv, qt, key_doc, row_doc, causal)
        weights = jnp.exp2(scores - norm_ref[0:1, lanes])
        grad_probs = nn(kv[:, HD:], dot)
        grad_scores = (weights * (grad_probs - norm_ref[1:2, lanes])).astype(BF16)
        dkt += nt(qt, grad_scores)
        dvt += nt(dot, weights.astype(BF16))
        dqt_ref[:, lanes] += tn(kv[:, :HD], grad_scores)
    return dkt, dvt


def place():
    srv = lax.axis_index("srv")
    return srv // 2, srv % 2


def reaches(ids_ref, rows, key_block, row_block):
    return ids_ref[key_block * rows + rows - 1] >= ids_ref[row_block * rows]


def pack_kernel(key_ref, value_ref, kv_ref):
    kv_ref[:, :HD] = key_ref[...]
    kv_ref[:, HD:] = value_ref[...]


def turn_kernel(q_ref, do_ref, after_ref, qd_ref):
    rows, columns = q_ref.shape
    for top, ref in ((0, q_ref), (HD, do_ref)):
        turned = jnp.transpose(ref[...])
        for head in range(columns // HD):
            qd_ref[top : top + HD, head * rows : (head + 1) * rows] = turned[
                head * HD : (head + 1) * HD, :
            ]


def own_stats_kernel(ids_ref, docs_ref, qd_own, qd_par, kv_ref, stats_ref):
    rows = docs_ref.shape[1]
    chip, core = place()
    stats_ref[...] = jnp.zeros(stats_ref.shape, F32)
    stats_ref[0:1, :] = jnp.full((1, stats_ref.shape[1]), LOWEST, F32)
    block = chip * 2 + core
    kv = kv_ref[...]
    add_stats(stats_ref, kv, qd_own, docs_ref, block, block, 0, True)
    other = chip * 2 + 1 - core

    @pl.when((core == 0) & reaches(ids_ref, rows, block, other))
    def _():
        add_stats(stats_ref, kv, qd_par, docs_ref, block, other, 1, False)


def each_remote(groups, ids_ref, rows, body):
    chip, core = place()

    def step(group, slot, away):
        source = chip ^ away
        key_block = source * 2 + core
        for side in range(2):
            row_block = chip * 2 + (core if side == 0 else 1 - core)
            active = (source < chip) & reaches(ids_ref, rows, key_block, row_block)
            pl.when(active)(functools.partial(body, group, slot, key_block, row_block, side))

    first = 1
    for group, amount in enumerate(groups):
        if amount == 1:
            step(group, 0, first)
        else:
            base = first

            @pl.loop(0, amount)
            def _(slot):
                step(group, slot, base + slot)

        first += amount


def far_stats_kernel(groups, ids_ref, docs_ref, qd_own, qd_par, stats_in, *rest):
    kv_refs, stats_ref = rest[:-1], rest[-1]
    rows = docs_ref.shape[1]
    stats_ref[...] = stats_in[...]

    def body(group, slot, key_block, row_block, side):
        qd_ref = (qd_own, qd_par)[side]
        kv = kv_refs[group][slot]
        add_stats(stats_ref, kv, qd_ref, docs_ref, key_block, row_block, side, False)

    each_remote(groups, ids_ref, rows, body)


def far_grads_kernel(groups, ids_ref, docs_ref, qd_own, qd_par, stats_ref, other_ref, *rest):
    count = len(groups)
    kv_refs, out_refs = rest[:count], rest[count : 2 * count]
    dqt_ref, norm_ref = rest[2 * count :]
    rows = docs_ref.shape[1]
    half = qd_own.shape[1]
    mine = stats_ref[...]
    other = other_ref[...]
    other = jnp.concatenate([other[:, half:], other[:, :half]], axis=1)
    top = jnp.maximum(mine[0:1], other[0:1])
    mine_by = jnp.exp2(mine[0:1] - top)
    other_by = jnp.exp2(other[0:1] - top)
    total = mine[1:2] * mine_by + other[1:2] * other_by
    norm_ref[...] = jnp.zeros(norm_ref.shape, F32)
    norm_ref[0:1, :] = top + jnp.log2(total)
    norm_ref[1:2, :] = (mine[2:3] * mine_by + other[2:3] * other_by) / total
    dqt_ref[...] = jnp.zeros(dqt_ref.shape, F32)
    for out_ref in out_refs:
        out_ref[...] = jnp.zeros(out_ref.shape, BF16)

    def body(group, slot, key_block, row_block, side):
        qd_ref = (qd_own, qd_par)[side]
        kv = kv_refs[group][slot]
        dkt, dvt = add_grads(
            kv, qd_ref, docs_ref, key_block, row_block, side, False, norm_ref, dqt_ref
        )
        both = jnp.concatenate([dkt * SCALE, dvt], axis=0)
        if side == 1:
            both = both + out_refs[group][slot].astype(F32)
        out_refs[group][slot] = both.astype(BF16)

    each_remote(groups, ids_ref, rows, body)


def own_grads_kernel(
    ids_ref, docs_ref, qd_own, qd_par, norm_ref, kv_ref, dqt_in, dkv_ref, dq_own, dq_par, dqt_ref
):
    rows = docs_ref.shape[1]
    heads = qd_own.shape[1] // rows
    chip, core = place()
    block = chip * 2 + core
    other = chip * 2 + 1 - core
    dqt_ref[...] = dqt_in[...]
    kv = kv_ref[...]
    dkt, dvt = add_grads(kv, qd_own, docs_ref, block, block, 0, True, norm_ref, dqt_ref)
    dkv_ref[...] = jnp.concatenate([dkt * SCALE, dvt], axis=0)

    @pl.when((core == 0) & reaches(ids_ref, rows, block, other))
    def _():
        dkt, dvt = add_grads(kv, qd_par, docs_ref, block, other, 1, False, norm_ref, dqt_ref)
        dkv_ref[...] += jnp.concatenate([dkt * SCALE, dvt], axis=0)

    for side, out_ref in enumerate((dq_own, dq_par)):
        for head in range(heads):
            chunk = side * heads + head
            out_ref[head * HD : (head + 1) * HD, :] = (
                dqt_ref[:, chunk * rows : (chunk + 1) * rows] * SCALE
            )


def query_kernel(dq_own, dq_far, dq_ref, token_ref):
    token_ref[...] = jnp.zeros(token_ref.shape, F32)
    dq_ref[...] = jnp.transpose(dq_own[...] + dq_far[...]).astype(BF16)


def combine_kernel(share, count, dq_in, own_ref, *rest):
    parts, outs = rest[:count], rest[count:]
    keep_ref, send_refs, sum_ref = outs[1], outs[2:-1], outs[-1]
    width = HD // share
    total = own_ref[...]
    for part in parts:
        for slot in range(part.shape[0]):
            total = total + part[slot].astype(F32)
    sum_ref[...] = total
    member = lax.axis_index("grp") % share
    for away, out_ref in enumerate((keep_ref, *send_refs)):
        first = pl.multiple_of((member ^ away) * width, width)
        for half in range(2):
            piece = sum_ref[pl.ds(half * HD + first, width), :]
            out_ref[half * width : (half + 1) * width, :] = piece.astype(out_ref.dtype)


def finish_kernel(after_ref, keep_ref, *rest):
    parts, (dk_ref, dv_ref) = rest[:-2], rest[-2:]
    total = keep_ref[...]
    for part in parts:
        total = total + part[...].astype(F32)
    width = total.shape[0] // 2
    dk_ref[...] = total[:width].astype(BF16)
    dv_ref[...] = total[width:].astype(BF16)


SMEM = pl.BlockSpec(memory_space=pltpu.SMEM)
VMEM = pl.BlockSpec(memory_space=pltpu.VMEM)
ANY = pl.BlockSpec(memory_space=pl.ANY)


def call(kernel, out_shape, operands, scratch=(), smem=0, unread=(), aliases={}, us=0):
    kinds = [SMEM] * smem + [VMEM] * (len(operands) - smem)
    results = [VMEM] * len(out_shape)
    for place_of in unread:
        kinds[place_of] = ANY
    for source, target in aliases.items():
        kinds[source] = ANY
        results[target] = ANY
    cost = pl.CostEstimate(flops=us * 10**9, bytes_accessed=1 << 19, transcendentals=0)
    return pl.pallas_call(
        kernel,
        out_shape=out_shape,
        in_specs=kinds,
        out_specs=results,
        scratch_shapes=list(scratch),
        input_output_aliases=aliases,
        cost_estimate=cost,
        compiler_params=pltpu.CompilerParams(vmem_limit_bytes=24 << 20),
    )(*operands)


def sds(shape, dtype):
    return jax.ShapeDtypeStruct(shape, dtype)


def on_device(queries, key_rows, value_rows, grad_output, doc_ids):
    rows, columns = queries.shape
    heads = columns // HD
    srv = lax.axis_size("srv")
    chips = srv // 2
    grp = lax.axis_size("grp")
    kv_heads = key_rows.shape[1] // HD
    share = grp // kv_heads
    lanes = 2 * heads * rows
    if kv_heads > 1:
        first = lax.axis_index("grp") // share * HD
        key_rows = lax.dynamic_slice_in_dim(key_rows, first, HD, 1)
        value_rows = lax.dynamic_slice_in_dim(value_rows, first, HD, 1)
    (own_kv,) = call(pack_kernel, [sds((rows, 2 * HD), BF16)], [key_rows, value_rows])
    docs = doc_ids.reshape(srv, rows)

    def trade(block, away):
        return lax.ppermute(block, "srv", [(i, i ^ 2 * away) for i in range(srv)])

    def swap(block):
        return lax.ppermute(block, "srv", [(i, i ^ 1) for i in range(srv)])

    far_kv = [trade(own_kv, away)[None] for away in range(chips - 1, 0, -1)][::-1]
    groups = [1] * len(far_kv)
    if chips > 4:
        groups = [len(far_kv)]
        far_kv = [jnp.concatenate(far_kv, axis=0)]
    (qd_own,) = call(
        turn_kernel,
        [sds((2 * HD, heads * rows), BF16)],
        [queries, grad_output, own_kv],
        unread=[2],
    )
    qd_par = swap(qd_own)
    shared = [doc_ids, docs, qd_own, qd_par]
    (stats,) = call(
        own_stats_kernel, [sds((8, lanes), F32)], [*shared, own_kv], smem=1
    )
    (stats,) = call(
        functools.partial(far_stats_kernel, groups),
        [sds((8, lanes), F32)],
        [*shared, stats, *far_kv],
        smem=1,
    )
    other_stats = swap(stats)
    *far_dkv, dqt, norm = call(
        functools.partial(far_grads_kernel, groups),
        [sds((amount, 2 * HD, rows), BF16) for amount in groups]
        + [sds((HD, lanes), F32), sds((8, lanes), F32)],
        [*shared, stats, other_stats, *far_kv],
        smem=1,
    )
    if chips > 4:
        far_dkv = [far_dkv[0][i : i + 1] for i in range(chips - 1)]
    came = [trade(part, away + 1) for away, part in enumerate(far_dkv)]
    own_dkv, dq_own, dq_par = call(
        own_grads_kernel,
        [sds((2 * HD, rows), F32)] + [sds((columns, rows), F32)] * 2,
        [*shared, norm, own_kv, dqt],
        scratch=[pltpu.VMEM((HD, lanes), F32)],
        smem=1,
        us=4,
    )
    width = HD // share
    dq_par, keep, *send = call(
        functools.partial(combine_kernel, share, len(came)),
        [sds(dq_par.shape, F32), sds((2 * width, rows), F32)]
        + [sds((2 * width, rows), BF16)] * (share - 1),
        [dq_par, own_dkv, *came],
        scratch=[pltpu.VMEM((2 * HD, rows), F32)],
        aliases={0: 0},
    )
    back = [
        lax.ppermute(part, "grp", [(i, i ^ (away + 1)) for i in range(grp)])
        for away, part in enumerate(send)
    ]
    grad_query, token = call(
        query_kernel,
        [sds((rows, columns), BF16), sds((8, 128), F32)],
        [dq_own, swap(dq_par)],
        us=2,
    )
    grad_key, grad_value = call(
        finish_kernel,
        [sds((width, rows), BF16)] * 2,
        [token, keep, *back],
        unread=[0],
    )
    return grad_query, grad_key.T, grad_value.T


def solution(mesh):
    in_specs = (P("srv", "grp"), P("srv", None), P("srv", None), P("srv", "grp"), P())
    out_specs = (P("srv", "grp"), P("srv", "grp"), P("srv", "grp"))
    return jax.shard_map(
        on_device, mesh=mesh, in_specs=in_specs, out_specs=out_specs, check_vma=False
    )
```

```python
import functools

import jax
import jax.numpy as jnp
from jax import lax
from jax.experimental import pallas as pl
from jax.experimental.pallas import tpu as pltpu
from jax.sharding import PartitionSpec as P

HD = 128
SCALE = HD**-0.5
LOG2E = 1.4426950408889634
MASKED = -1.0e30
LOWEST = -1.0e20
F32 = jnp.float32
BF16 = jnp.bfloat16


def nn(a, b):
    return lax.dot_general(a, b, (((1,), (0,)), ((), ())), preferred_element_type=F32)


def nt(a, b):
    return lax.dot_general(a, b, (((1,), (1,)), ((), ())), preferred_element_type=F32)


def tn(a, b):
    return lax.dot_general(a, b, (((0,), (0,)), ((), ())), preferred_element_type=F32)


def key_doc_column(docs_ref, block):
    row = docs_ref[pl.ds(block, 1), :]
    span = row.shape[1]
    column = jnp.transpose(jnp.broadcast_to(row, (128, span)))
    return jnp.concatenate([column] * (span // 128), axis=1)


def scores_of(kv, qt, key_doc, row_doc, causal):
    scores = nn(kv[:, :HD], qt) * (SCALE * LOG2E)
    allowed = key_doc == row_doc
    if causal:
        key_pos = lax.broadcasted_iota(jnp.int32, scores.shape, 0)
        row_pos = lax.broadcasted_iota(jnp.int32, scores.shape, 1)
        allowed = allowed & (key_pos <= row_pos)
    return jnp.where(allowed, scores, MASKED)


def add_stats(stats_ref, kv, qd_ref, docs_ref, key_block, row_block, side, causal):
    rows = docs_ref.shape[1]
    key_doc = key_doc_column(docs_ref, key_block)
    row_doc = docs_ref[pl.ds(row_block, 1), :]
    heads = qd_ref.shape[1] // rows
    for head in range(heads):
        local = slice(head * rows, (head + 1) * rows)
        lanes = slice((side * heads + head) * rows, (side * heads + head + 1) * rows)
        scores = scores_of(kv, qd_ref[:HD, local], key_doc, row_doc, causal)
        grad_probs = nn(kv[:, HD:], qd_ref[HD:, local])
        old = stats_ref[0:1, lanes]
        new = jnp.maximum(old, jnp.max(scores, axis=0, keepdims=True))
        factor = jnp.exp2(old - new)
        weights = jnp.exp2(scores - new)
        stats_ref[0:1, lanes] = new
        stats_ref[1:2, lanes] = stats_ref[1:2, lanes] * factor + jnp.sum(
            weights, axis=0, keepdims=True
        )
        stats_ref[2:3, lanes] = stats_ref[2:3, lanes] * factor + jnp.sum(
            weights * grad_probs, axis=0, keepdims=True
        )


def add_grads(kv, qd_ref, docs_ref, key_block, row_block, side, causal, norm_ref, dqt_ref):
    rows = docs_ref.shape[1]
    key_doc = key_doc_column(docs_ref, key_block)
    row_doc = docs_ref[pl.ds(row_block, 1), :]
    dkt = jnp.zeros((HD, rows), F32)
    dvt = jnp.zeros((HD, rows), F32)
    heads = qd_ref.shape[1] // rows
    for head in range(heads):
        local = slice(head * rows, (head + 1) * rows)
        lanes = slice((side * heads + head) * rows, (side * heads + head + 1) * rows)
        qt = qd_ref[:HD, local]
        dot = qd_ref[HD:, local]
        scores = scores_of(kv, qt, key_doc, row_doc, causal)
        weights = jnp.exp2(scores - norm_ref[0:1, lanes])
        grad_probs = nn(kv[:, HD:], dot)
        grad_scores = (weights * (grad_probs - norm_ref[1:2, lanes])).astype(BF16)
        dkt += nt(qt, grad_scores)
        dvt += nt(dot, weights.astype(BF16))
        dqt_ref[:, lanes] += tn(kv[:, :HD], grad_scores)
    return dkt, dvt


def place():
    srv = lax.axis_index("srv")
    return srv // 2, srv % 2


def reaches(docs_ref, key_block, row_block):
    last = docs_ref[pl.ds(key_block, 1), :][0, docs_ref.shape[1] - 1]
    return last >= docs_ref[pl.ds(row_block, 1), :][0, 0]


def pack_kernel(key_ref, value_ref, kv_ref, sems):
    copies = [
        pltpu.make_async_copy(ref, kv_ref.at[:, half * HD : (half + 1) * HD], sems.at[half])
        for half, ref in enumerate((key_ref, value_ref))
    ]
    for copy in copies:
        copy.start()
    for copy in copies:
        copy.wait()


def turn_kernel(q_ref, do_ref, after_ref, qd_ref):
    rows, columns = q_ref.shape
    for top, ref in ((0, q_ref), (HD, do_ref)):
        turned = jnp.transpose(ref[...])
        for head in range(columns // HD):
            qd_ref[top : top + HD, head * rows : (head + 1) * rows] = turned[
                head * HD : (head + 1) * HD, :
            ]


def own_stats_kernel(docs_ref, qd_own, qd_par, kv_ref, stats_ref):
    rows = docs_ref.shape[1]
    chip, core = place()
    stats_ref[...] = jnp.zeros(stats_ref.shape, F32)
    stats_ref[0:1, :] = jnp.full((1, stats_ref.shape[1]), LOWEST, F32)
    block = chip * 2 + core
    kv = kv_ref[...]
    add_stats(stats_ref, kv, qd_own, docs_ref, block, block, 0, True)
    other = chip * 2 + 1 - core

    @pl.when((core == 0) & reaches(docs_ref, block, other))
    def _():
        add_stats(stats_ref, kv, qd_par, docs_ref, block, other, 1, False)


def each_remote(first, count, docs_ref, body):
    chip, core = place()

    def step(slot):
        source = chip ^ (first + slot)
        key_block = source * 2 + core
        for side in range(2):
            row_block = chip * 2 + (core if side == 0 else 1 - core)
            active = (source < chip) & reaches(docs_ref, key_block, row_block)
            pl.when(active)(functools.partial(body, slot, key_block, row_block, side))

    if count == 1:
        step(0)
    else:
        pl.loop(0, count)(step)


def far_stats_kernel(first, docs_ref, qd_own, qd_par, stats_in, kv_ref, stats_ref):
    stats_ref[...] = stats_in[...]

    def body(slot, key_block, row_block, side):
        qd_ref = (qd_own, qd_par)[side]
        add_stats(stats_ref, kv_ref[slot], qd_ref, docs_ref, key_block, row_block, side, False)

    each_remote(first, kv_ref.shape[0], docs_ref, body)


def norm_kernel(stats_ref, other_ref, norm_ref):
    half = stats_ref.shape[1] // 2
    mine = stats_ref[...]
    other = other_ref[...]
    other = jnp.concatenate([other[:, half:], other[:, :half]], axis=1)
    top = jnp.maximum(mine[0:1], other[0:1])
    mine_by = jnp.exp2(mine[0:1] - top)
    other_by = jnp.exp2(other[0:1] - top)
    total = mine[1:2] * mine_by + other[1:2] * other_by
    norm_ref[...] = jnp.zeros(norm_ref.shape, F32)
    norm_ref[0:1, :] = top + jnp.log2(total)
    norm_ref[1:2, :] = (mine[2:3] * mine_by + other[2:3] * other_by) / total


def far_grads_kernel(first, docs_ref, qd_own, qd_par, norm_ref, kv_ref, out_ref, dqt_ref):
    dqt_ref[...] = jnp.zeros(dqt_ref.shape, F32)
    out_ref[...] = jnp.zeros(out_ref.shape, BF16)

    def body(slot, key_block, row_block, side):
        qd_ref = (qd_own, qd_par)[side]
        dkt, dvt = add_grads(
            kv_ref[slot], qd_ref, docs_ref, key_block, row_block, side, False, norm_ref, dqt_ref
        )
        both = jnp.concatenate([dkt * SCALE, dvt], axis=0)
        if side == 1:
            both = both + out_ref[slot].astype(F32)
        out_ref[slot] = both.astype(BF16)

    each_remote(first, kv_ref.shape[0], docs_ref, body)


def own_grads_kernel(docs_ref, qd_own, qd_par, norm_ref, kv_ref, *rest):
    dqt_in, (dkv_ref, dq_own, dq_par, dqt_ref) = rest[:-4], rest[-4:]
    rows = docs_ref.shape[1]
    heads = qd_own.shape[1] // rows
    chip, core = place()
    block = chip * 2 + core
    other = chip * 2 + 1 - core
    dqt_ref[...] = sum(part[...] for part in dqt_in)
    kv = kv_ref[...]
    dkt, dvt = add_grads(kv, qd_own, docs_ref, block, block, 0, True, norm_ref, dqt_ref)
    dkv_ref[...] = jnp.concatenate([dkt * SCALE, dvt], axis=0)

    @pl.when((core == 0) & reaches(docs_ref, block, other))
    def _():
        dkt, dvt = add_grads(kv, qd_par, docs_ref, block, other, 1, False, norm_ref, dqt_ref)
        dkv_ref[...] += jnp.concatenate([dkt * SCALE, dvt], axis=0)

    for side, out_ref in enumerate((dq_own, dq_par)):
        for head in range(heads):
            chunk = side * heads + head
            out_ref[head * HD : (head + 1) * HD, :] = (
                dqt_ref[:, chunk * rows : (chunk + 1) * rows] * SCALE
            )


def query_kernel(dq_own, dq_far, dq_ref, token_ref):
    token_ref[...] = jnp.zeros(token_ref.shape, F32)
    dq_ref[...] = jnp.transpose(dq_own[...] + dq_far[...]).astype(BF16)


def combine_kernel(share, count, dq_in, own_ref, *rest):
    parts, outs = rest[:count], rest[count:]
    keep_ref, send_refs, sum_ref = outs[1], outs[2:-1], outs[-1]
    width = HD // share
    total = own_ref[...]
    for part in parts:
        total = total + part[...].astype(F32)
    sum_ref[...] = total
    member = lax.axis_index("grp") % share
    for away, out_ref in zip((0, *range(share - 1, 0, -1)), (keep_ref, *send_refs)):
        first = pl.multiple_of((member ^ away) * width, width)
        for half in range(2):
            piece = sum_ref[pl.ds(half * HD + first, width), :]
            out_ref[half * width : (half + 1) * width, :] = piece.astype(out_ref.dtype)


def finish_kernel(after_ref, keep_ref, *rest):
    parts, (dk_ref, dv_ref) = rest[:-2], rest[-2:]
    total = keep_ref[...]
    for part in parts:
        total = total + part[...].astype(F32)
    width = total.shape[0] // 2
    dk_ref[...] = total[:width].astype(BF16)
    dv_ref[...] = total[width:].astype(BF16)


VMEM = pl.BlockSpec(memory_space=pltpu.VMEM)
ANY = pl.BlockSpec(memory_space=pl.ANY)


HBM = pl.BlockSpec(memory_space=pltpu.HBM)


def call(kernel, out_shape, operands, scratch=(), unread=(), aliases={}, us=0, hbm=0, vmem=24):
    kinds = [HBM] * hbm + [VMEM] * (len(operands) - hbm)
    results = [VMEM] * len(out_shape)
    for place_of in unread:
        kinds[place_of] = ANY
    for source, target in aliases.items():
        kinds[source] = ANY
        results[target] = ANY
    cost = pl.CostEstimate(flops=us * 10**9, bytes_accessed=1 << 19, transcendentals=0)
    return pl.pallas_call(
        kernel,
        out_shape=out_shape,
        in_specs=kinds,
        out_specs=results,
        scratch_shapes=list(scratch),
        input_output_aliases=aliases,
        cost_estimate=cost,
        compiler_params=pltpu.CompilerParams(vmem_limit_bytes=vmem << 20),
    )(*operands)


def sds(shape, dtype):
    return jax.ShapeDtypeStruct(shape, dtype)


def on_device(queries, key_rows, value_rows, grad_output, doc_ids):
    rows, columns = queries.shape
    heads = columns // HD
    srv = lax.axis_size("srv")
    chips = srv // 2
    grp = lax.axis_size("grp")
    kv_heads = key_rows.shape[1] // HD
    share = grp // kv_heads
    lanes = 2 * heads * rows
    if kv_heads > 1:
        first = lax.axis_index("grp") // share * HD
        key_rows = lax.dynamic_slice_in_dim(key_rows, first, HD, 1)
        value_rows = lax.dynamic_slice_in_dim(value_rows, first, HD, 1)
    (own_kv,) = call(
        pack_kernel,
        [sds((rows, 2 * HD), BF16)],
        [key_rows, value_rows],
        scratch=[pltpu.SemaphoreType.DMA((2,))],
        hbm=2,
        vmem=60,
    )
    docs = doc_ids.reshape(srv, rows)

    def trade(block, away):
        return lax.ppermute(block, "srv", [(i, i ^ 2 * away) for i in range(srv)])

    def swap(block):
        return lax.ppermute(block, "srv", [(i, i ^ 1) for i in range(srv)])

    order = list(range(chips - 1, 0, -1))
    far_kv = {away: trade(own_kv, away)[None] for away in order}
    if chips > 4:
        far_kv = {1: jnp.concatenate([far_kv[away] for away in order[::-1]], axis=0)}
    (qd_own,) = call(
        turn_kernel,
        [sds((2 * HD, heads * rows), BF16)],
        [queries, grad_output, own_kv],
        unread=[2],
    )
    qd_par = swap(qd_own)
    shared = [docs, qd_own, qd_par]
    (stats,) = call(
        own_stats_kernel, [sds((8, lanes), F32)], [*shared, own_kv]
    )
    for first, kv in far_kv.items():
        (stats,) = call(
            functools.partial(far_stats_kernel, first),
            [sds((8, lanes), F32)],
            [*shared, stats, kv],
            )
    (norm,) = call(norm_kernel, [sds((8, lanes), F32)], [stats, swap(stats)])
    came, dqt = [], []
    for first, kv in far_kv.items():
        part, dqt_part = call(
            functools.partial(far_grads_kernel, first),
            [sds(kv.shape[:1] + (2 * HD, rows), BF16), sds((HD, lanes), F32)],
            [*shared, norm, kv],
            )
        dqt.append(dqt_part)
        came += [trade(part[slot], first + slot) for slot in range(kv.shape[0])]
    own_dkv, dq_own, dq_par = call(
        own_grads_kernel,
        [sds((2 * HD, rows), F32)] + [sds((columns, rows), F32)] * 2,
        [*shared, norm, own_kv, *dqt],
        scratch=[pltpu.VMEM((HD, lanes), F32)],
        us=4,
    )
    width = HD // share
    dq_par, keep, *send = call(
        functools.partial(combine_kernel, share, len(came)),
        [sds(dq_par.shape, F32), sds((2 * width, rows), F32)]
        + [sds((2 * width, rows), BF16)] * (share - 1),
        [dq_par, own_dkv, *came],
        scratch=[pltpu.VMEM((2 * HD, rows), F32)],
        aliases={0: 0},
    )
    back = [
        lax.ppermute(part, "grp", [(i, i ^ away) for i in range(grp)])
        for away, part in zip(range(share - 1, 0, -1), send)
    ]
    grad_query, token = call(
        query_kernel,
        [sds((rows, columns), BF16), sds((8, 128), F32)],
        [dq_own, swap(dq_par)],
        us=2,
    )
    grad_key, grad_value = call(
        finish_kernel,
        [sds((width, rows), BF16)] * 2,
        [token, keep, *back],
        unread=[0],
    )
    return grad_query, grad_key.T, grad_value.T


def solution(mesh):
    in_specs = (P("srv", "grp"), P("srv", None), P("srv", None), P("srv", "grp"), P())
    out_specs = (P("srv", "grp"), P("srv", "grp"), P("srv", "grp"))
    return jax.shard_map(
        on_device, mesh=mesh, in_specs=in_specs, out_specs=out_specs, check_vma=False
    )
```

```python
import functools

import jax
import jax.numpy as jnp
from jax import lax
from jax.experimental import pallas as pl
from jax.experimental.pallas import tpu as pltpu
from jax.sharding import PartitionSpec as P

HD = 128
SCALE = HD**-0.5
LOG2E = 1.4426950408889634
MASKED = -1.0e30
LOWEST = -1.0e20
F32 = jnp.float32
BF16 = jnp.bfloat16


def nn(a, b):
    return lax.dot_general(a, b, (((1,), (0,)), ((), ())), preferred_element_type=F32)


def nt(a, b):
    return lax.dot_general(a, b, (((1,), (1,)), ((), ())), preferred_element_type=F32)


def tn(a, b):
    return lax.dot_general(a, b, (((0,), (0,)), ((), ())), preferred_element_type=F32)


def place():
    srv = lax.axis_index("srv")
    return srv // 2, srv % 2


def hot_kernel(docs_ref, khot_ref, rhot_ref):
    rows = docs_ref.shape[1]
    chip, core = place()
    kind = lax.broadcasted_iota(jnp.int32, (HD, rows), 0)
    for source in range(khot_ref.shape[0]):
        hot = kind == docs_ref[pl.ds(source * 2 + core, 1), :]
        khot_ref[source] = jnp.transpose(hot.astype(F32)).astype(BF16)
    for side in range(2):
        row_block = chip * 2 + (core if side == 0 else 1 - core)
        hot = kind == docs_ref[pl.ds(row_block, 1), :]
        rhot_ref[:, side * rows : (side + 1) * rows] = jnp.where(hot, 0.0, MASKED).astype(BF16)


def chunks_of(sides, qds, rhot_ref):
    rows = rhot_ref.shape[1] // 2
    heads = qds[0].shape[1] // rows
    for side in sides:
        for head in range(heads):
            local = slice(head * rows, (head + 1) * rows)
            chunk = side * heads + head
            lanes = slice(chunk * rows, (chunk + 1) * rows)
            penalty = rhot_ref[:, side * rows : (side + 1) * rows]
            yield lanes, qds[side][:HD, local], qds[side][HD:, local], penalty


def scores_of(kv, khot, qt, penalty, causal):
    keys = jnp.concatenate([kv[:, :HD], khot], axis=1)
    scores = nn(keys, jnp.concatenate([qt, penalty], axis=0))
    if causal:
        key_pos = lax.broadcasted_iota(jnp.int32, scores.shape, 0)
        row_pos = lax.broadcasted_iota(jnp.int32, scores.shape, 1)
        scores = jnp.where(key_pos <= row_pos, scores, MASKED)
    return scores


def add_stats(stats_ref, kv, khot, qds, rhot_ref, sides, causal):
    for lanes, qt, dot, penalty in chunks_of(sides, qds, rhot_ref):
        scores = scores_of(kv, khot, qt, penalty, causal)
        grad_probs = nn(kv[:, HD:], dot)
        old = stats_ref[0:1, lanes]
        new = jnp.maximum(old, jnp.max(scores, axis=0, keepdims=True) * (SCALE * LOG2E))
        factor = jnp.exp2(old - new)
        weights = jnp.exp2(scores * (SCALE * LOG2E) - new)
        stats_ref[0:1, lanes] = new
        stats_ref[1:2, lanes] = stats_ref[1:2, lanes] * factor + jnp.sum(
            weights, axis=0, keepdims=True
        )
        stats_ref[2:3, lanes] = stats_ref[2:3, lanes] * factor + jnp.sum(
            weights * grad_probs, axis=0, keepdims=True
        )


def add_grads(kv, khot, qds, rhot_ref, sides, causal, norm_ref, dqt_ref, fresh):
    qts, dots, lows, grads = [], [], [], []
    for lanes, qt, dot, penalty in chunks_of(sides, qds, rhot_ref):
        scores = scores_of(kv, khot, qt, penalty, causal)
        weights = jnp.exp2(scores * (SCALE * LOG2E) - norm_ref[0:1, lanes])
        grad_probs = nn(kv[:, HD:], dot)
        grad_scores = (weights * (grad_probs - norm_ref[1:2, lanes])).astype(BF16)
        change = tn(kv[:, :HD], grad_scores)
        if fresh:
            dqt_ref[:, lanes] = change
        else:
            dqt_ref[:, lanes] += change
        qts.append(qt)
        dots.append(dot)
        lows.append(weights.astype(BF16))
        grads.append(grad_scores)

    def joined(parts):
        return jnp.concatenate(parts, axis=1)

    dkt = nt(joined(qts), joined(grads)) * SCALE
    dvt = nt(joined(dots), joined(lows))
    return jnp.concatenate([dkt, dvt], axis=0)


def reaches(docs_ref, key_block, row_block):
    last = docs_ref[pl.ds(key_block, 1), :][0, docs_ref.shape[1] - 1]
    return last >= docs_ref[pl.ds(row_block, 1), :][0, 0]


def blank_kernel(stats_ref):
    stats_ref[...] = jnp.zeros(stats_ref.shape, F32)
    stats_ref[0:1, :] = jnp.full((1, stats_ref.shape[1]), LOWEST, F32)


def pack_kernel(after_ref, key_ref, value_ref, kv_ref):
    kv_ref[:, :HD] = key_ref[...]
    kv_ref[:, HD:] = value_ref[...]


def turn_kernel(q_own, do_own, q_par, do_par, qd_own, qd_par):
    rows, columns = q_own.shape
    for q_ref, do_ref, qd_ref in ((q_own, do_own, qd_own), (q_par, do_par, qd_par)):
        for top, ref in ((0, q_ref), (HD, do_ref)):
            turned = jnp.transpose(ref[...])
            for head in range(columns // HD):
                qd_ref[top : top + HD, head * rows : (head + 1) * rows] = turned[
                    head * HD : (head + 1) * HD, :
                ]


def own_stats_kernel(khot_ref, rhot_ref, qd_own, qd_par, kv_ref, stats_in, stats_ref):
    chip, core = place()
    stats_ref[...] = stats_in[...]
    kv, khot, qds = kv_ref[...], khot_ref[chip], (qd_own, qd_par)
    add_stats(stats_ref, kv, khot, qds, rhot_ref, (0,), True)

    @pl.when(core == 0)
    def _():
        add_stats(stats_ref, kv, khot, qds, rhot_ref, (1,), False)


def each_remote(first, kv_ref, docs_ref, body, rest):
    chip, core = place()
    count = kv_ref.shape[0]

    def step(slot):
        source = chip ^ (first + slot)

        @pl.when(source < chip)
        def _():
            active = reaches(docs_ref, source * 2 + core, chip * 2)
            pl.when(active)(functools.partial(body, slot, source))
            if rest is not None:
                pl.when(jnp.logical_not(active))(rest)

        if rest is not None:
            pl.when(source > chip)(rest)

    if count == 1:
        step(0)
    else:
        pl.loop(0, count)(step)


def far_stats_kernel(firsts, docs_ref, khot_ref, rhot_ref, qd_own, qd_par, stats_in, *rest):
    kv_refs, stats_ref = rest[:-1], rest[-1]
    stats_ref[...] = stats_in[...]
    qds = qd_own, qd_par
    for first, kv_ref in zip(firsts, kv_refs):

        def body(slot, source, kv_ref=kv_ref):
            add_stats(stats_ref, kv_ref[slot], khot_ref[source], qds, rhot_ref, (0, 1), False)

        each_remote(first, kv_ref, docs_ref, body, None)


def norm_kernel(stats_ref, other_ref, norm_ref):
    half = stats_ref.shape[1] // 2
    mine = stats_ref[...]
    other = other_ref[...]
    other = jnp.concatenate([other[:, half:], other[:, :half]], axis=1)
    top = jnp.maximum(mine[0:1], other[0:1])
    mine_by = jnp.exp2(mine[0:1] - top)
    other_by = jnp.exp2(other[0:1] - top)
    total = mine[1:2] * mine_by + other[1:2] * other_by
    norm_ref[...] = jnp.zeros(norm_ref.shape, F32)
    norm_ref[0:1, :] = top + jnp.log2(total)
    norm_ref[1:2, :] = (mine[2:3] * mine_by + other[2:3] * other_by) / total


def far_grads_kernel(
    first, docs_ref, khot_ref, rhot_ref, qd_own, qd_par, norm_ref, kv_ref, out_ref, dqt_ref
):
    alone = kv_ref.shape[0] == 1
    qds = qd_own, qd_par

    def clear():
        dqt_ref[...] = jnp.zeros(dqt_ref.shape, F32)
        out_ref[...] = jnp.zeros(out_ref.shape, BF16)

    if not alone:
        clear()

    def body(slot, source):
        part = add_grads(
            kv_ref[slot], khot_ref[source], qds, rhot_ref, (0, 1), False, norm_ref, dqt_ref, alone
        )
        out_ref[slot] = part.astype(BF16)

    each_remote(first, kv_ref, docs_ref, body, clear if alone else None)


def own_grads_kernel(after_ref, khot_ref, rhot_ref, qd_own, qd_par, norm_ref, kv_ref, *rest):
    dqt_in, (dkv_ref, dq_own, dq_par, dqt_ref) = rest[:-4], rest[-4:]
    rows = kv_ref.shape[0]
    heads = qd_own.shape[1] // rows
    chip, core = place()
    dqt_ref[...] = sum(part[...] for part in dqt_in)
    kv, khot, qds = kv_ref[...], khot_ref[chip], (qd_own, qd_par)
    dkv_ref[...] = add_grads(kv, khot, qds, rhot_ref, (0,), True, norm_ref, dqt_ref, False)

    @pl.when(core == 0)
    def _():
        dkv_ref[...] += add_grads(kv, khot, qds, rhot_ref, (1,), False, norm_ref, dqt_ref, False)

    for side, out_ref in enumerate((dq_own, dq_par)):
        for head in range(heads):
            chunk = side * heads + head
            out_ref[head * HD : (head + 1) * HD, :] = (
                dqt_ref[:, chunk * rows : (chunk + 1) * rows] * SCALE
            )


def query_kernel(dq_own, dq_far, dq_ref, token_ref):
    token_ref[...] = jnp.zeros(token_ref.shape, F32)
    dq_ref[...] = jnp.transpose(dq_own[...] + dq_far[...]).astype(BF16)


def combine_kernel(share, count, dq_in, own_ref, *rest):
    parts, outs = rest[:count], rest[count:]
    keep_ref, send_refs, sum_ref = outs[1], outs[2:-1], outs[-1]
    width = HD // share
    total = own_ref[...]
    for part in parts:
        total = total + part[...].astype(F32)
    sum_ref[...] = total
    member = lax.axis_index("grp") % share
    for away, out_ref in zip((0, *range(share - 1, 0, -1)), (keep_ref, *send_refs)):
        first = pl.multiple_of((member ^ away) * width, width)
        for half in range(2):
            piece = sum_ref[pl.ds(half * HD + first, width), :]
            out_ref[half * width : (half + 1) * width, :] = piece.astype(out_ref.dtype)


def finish_kernel(after_ref, keep_ref, *rest):
    parts, (dk_ref, dv_ref) = rest[:-2], rest[-2:]
    total = keep_ref[...]
    for part in parts:
        total = total + part[...].astype(F32)
    width = total.shape[0] // 2
    dk_ref[...] = total[:width].astype(BF16)
    dv_ref[...] = total[width:].astype(BF16)


VMEM = pl.BlockSpec(memory_space=pltpu.VMEM)
ANY = pl.BlockSpec(memory_space=pl.ANY)


HBM = pl.BlockSpec(memory_space=pltpu.HBM)


def call(kernel, out_shape, operands, scratch=(), unread=(), aliases={}, us=0, hbm=0, vmem=24):
    kinds = [HBM] * hbm + [VMEM] * (len(operands) - hbm)
    results = [VMEM] * len(out_shape)
    for place_of in unread:
        kinds[place_of] = ANY
    for source, target in aliases.items():
        kinds[source] = ANY
        results[target] = ANY
    cost = pl.CostEstimate(flops=us * 10**9, bytes_accessed=1 << 19, transcendentals=0)
    return pl.pallas_call(
        kernel,
        out_shape=out_shape,
        in_specs=kinds,
        out_specs=results,
        scratch_shapes=list(scratch),
        input_output_aliases=aliases,
        cost_estimate=cost,
        compiler_params=pltpu.CompilerParams(vmem_limit_bytes=vmem << 20),
    )(*operands)


def sds(shape, dtype):
    return jax.ShapeDtypeStruct(shape, dtype)


def on_device(queries, key_rows, value_rows, grad_output, doc_ids):
    rows, columns = queries.shape
    heads = columns // HD
    srv = lax.axis_size("srv")
    chips = srv // 2
    grp = lax.axis_size("grp")
    kv_heads = key_rows.shape[1] // HD
    share = grp // kv_heads
    lanes = 2 * heads * rows
    if kv_heads > 1:
        first = lax.axis_index("grp") // share * HD
        key_rows = lax.dynamic_slice_in_dim(key_rows, first, HD, 1)
        value_rows = lax.dynamic_slice_in_dim(value_rows, first, HD, 1)
    (blank,) = call(blank_kernel, [sds((8, lanes), F32)], [], us=5)
    (own_kv,) = call(
        pack_kernel,
        [sds((rows, 2 * HD), BF16)],
        [blank, key_rows, value_rows],
        unread=[0],
    )
    docs = doc_ids.reshape(srv, rows)

    def trade(block, away):
        return lax.ppermute(block, "srv", [(i, i ^ 2 * away) for i in range(srv)])

    def swap(block):
        return lax.ppermute(block, "srv", [(i, i ^ 1) for i in range(srv)])

    order = list(range(chips - 1, 0, -1))
    far_kv = {away: trade(own_kv, away)[None] for away in order}
    if chips > 4:
        far_kv = {1: jnp.concatenate([far_kv[away] for away in order[::-1]], axis=0)}
    qd_own, qd_par = call(
        turn_kernel,
        [sds((2 * HD, heads * rows), BF16)] * 2,
        [queries, grad_output, swap(queries), swap(grad_output)],
    )
    khot, rhot = call(
        hot_kernel,
        [sds((chips, rows, HD), BF16), sds((HD, 2 * rows), BF16)],
        [docs],
    )
    shared = [docs, khot, rhot, qd_own, qd_par]
    (stats,) = call(
        own_stats_kernel, [sds((8, lanes), F32)], [*shared[1:], own_kv, blank]
    )
    for firsts in (list(far_kv)[:1], list(far_kv)[1:]):
        if firsts:
            (stats,) = call(
                functools.partial(far_stats_kernel, firsts),
                [sds((8, lanes), F32)],
                [*shared, stats, *[far_kv[first] for first in firsts]],
            )
    (norm,) = call(norm_kernel, [sds((8, lanes), F32)], [stats, swap(stats)])
    came, dqt = [], []
    for first, kv in reversed(far_kv.items()):
        part, dqt_part = call(
            functools.partial(far_grads_kernel, first),
            [sds(kv.shape[:1] + (2 * HD, rows), BF16), sds((HD, lanes), F32)],
            [*shared, norm, kv],
            )
        dqt.append(dqt_part)
        came += [trade(part[slot], first + slot) for slot in range(kv.shape[0])]
    own_dkv, dq_own, dq_par = call(
        own_grads_kernel,
        [sds((2 * HD, rows), F32)] + [sds((columns, rows), F32)] * 2,
        [came[-1], *shared[1:], norm, own_kv, *dqt],
        scratch=[pltpu.VMEM((HD, lanes), F32)],
        unread=[0],
        us=4,
    )
    width = HD // share
    dq_par, keep, *send = call(
        functools.partial(combine_kernel, share, len(came)),
        [sds(dq_par.shape, F32), sds((2 * width, rows), F32)]
        + [sds((2 * width, rows), BF16)] * (share - 1),
        [dq_par, own_dkv, *came],
        scratch=[pltpu.VMEM((2 * HD, rows), F32)],
        aliases={0: 0},
    )
    back = [
        lax.ppermute(part, "grp", [(i, i ^ away) for i in range(grp)])
        for away, part in zip(range(share - 1, 0, -1), send)
    ]
    grad_query, token = call(
        query_kernel,
        [sds((rows, columns), BF16), sds((8, 128), F32)],
        [dq_own, swap(dq_par)],
        us=2,
    )
    grad_key, grad_value = call(
        finish_kernel,
        [sds((width, rows), BF16)] * 2,
        [token, keep, *back],
        unread=[0],
    )
    return grad_query, grad_key.T, grad_value.T


def solution(mesh):
    in_specs = (P("srv", "grp"), P("srv", None), P("srv", None), P("srv", "grp"), P())
    out_specs = (P("srv", "grp"), P("srv", "grp"), P("srv", "grp"))
    return jax.shard_map(
        on_device, mesh=mesh, in_specs=in_specs, out_specs=out_specs, check_vma=False
    )
```

```python
import functools

import jax
import jax.numpy as jnp
from jax import lax
from jax.experimental import pallas as pl
from jax.experimental.pallas import tpu as pltpu
from jax.sharding import PartitionSpec as P

HD = 128
SCALE = HD**-0.5
LOG2E = 1.4426950408889634
MASKED = -1.0e30
LOWEST = -1.0e20
DOC_MOST = {2048: 1280, 8192: 4352}
CORNER = [(1, 7), (7, 6), (6, 2), (2, 4), (4, 0), (0, 1), (3, 5), (5, 3)]
F32 = jnp.float32
BF16 = jnp.bfloat16


def nn(a, b):
    return lax.dot_general(a, b, (((1,), (0,)), ((), ())), preferred_element_type=F32)


def nt(a, b):
    return lax.dot_general(a, b, (((1,), (1,)), ((), ())), preferred_element_type=F32)


def tn(a, b):
    return lax.dot_general(a, b, (((0,), (0,)), ((), ())), preferred_element_type=F32)


def place():
    srv = lax.axis_index("srv")
    return srv // 2, srv % 2


def hot_kernel(docs_ref, khot_ref, rhot_ref):
    rows = docs_ref.shape[1]
    chip, core = place()
    kind = lax.broadcasted_iota(jnp.int32, (HD, rows), 0)
    for source in range(khot_ref.shape[0]):
        hot = kind == docs_ref[pl.ds(source * 2 + core, 1), :]
        khot_ref[source] = jnp.transpose(hot.astype(F32)).astype(BF16)
    for side in range(2):
        row_block = chip * 2 + (core if side == 0 else 1 - core)
        hot = kind == docs_ref[pl.ds(row_block, 1), :]
        rhot_ref[:, side * rows : (side + 1) * rows] = jnp.where(hot, 0.0, MASKED).astype(BF16)


def chunks_of(sides, qds, rhot_ref):
    rows = rhot_ref.shape[1] // 2
    heads = qds[0].shape[1] // rows
    for side in sides:
        for head in range(heads):
            local = slice(head * rows, (head + 1) * rows)
            chunk = side * heads + head
            lanes = slice(chunk * rows, (chunk + 1) * rows)
            penalty = rhot_ref[:, side * rows : (side + 1) * rows]
            yield lanes, qds[side][:HD, local], qds[side][HD:, local], penalty


def scores_of(kv, khot, qt, penalty, causal):
    keys = jnp.concatenate([kv[:, :HD], khot], axis=1)
    scores = nn(keys, jnp.concatenate([qt, penalty], axis=0))
    if causal:
        key_pos = lax.broadcasted_iota(jnp.int32, scores.shape, 0)
        row_pos = lax.broadcasted_iota(jnp.int32, scores.shape, 1)
        scores = jnp.where(key_pos <= row_pos, scores, MASKED)
    return scores


def add_stats(stats_ref, kv, khot, qds, rhot_ref, sides, causal):
    for lanes, qt, dot, penalty in chunks_of(sides, qds, rhot_ref):
        scores = scores_of(kv, khot, qt, penalty, causal)
        grad_probs = nn(kv[:, HD:], dot)
        old = stats_ref[0:1, lanes]
        new = jnp.maximum(old, jnp.max(scores, axis=0, keepdims=True) * (SCALE * LOG2E))
        factor = jnp.exp2(old - new)
        weights = jnp.exp2(scores * (SCALE * LOG2E) - new)
        stats_ref[0:1, lanes] = new
        stats_ref[1:2, lanes] = stats_ref[1:2, lanes] * factor + jnp.sum(
            weights, axis=0, keepdims=True
        )
        stats_ref[2:3, lanes] = stats_ref[2:3, lanes] * factor + jnp.sum(
            weights * grad_probs, axis=0, keepdims=True
        )


def add_grads(kv, khot, qds, rhot_ref, sides, causal, norm_ref, dqt_ref, fresh):
    qts, dots, lows, grads, all_lanes = [], [], [], [], []
    for lanes, qt, dot, penalty in chunks_of(sides, qds, rhot_ref):
        scores = scores_of(kv, khot, qt, penalty, causal)
        weights = jnp.exp2(scores * (SCALE * LOG2E) - norm_ref[0:1, lanes])
        grad_probs = nn(kv[:, HD:], dot)
        grad_scores = (weights * (grad_probs - norm_ref[1:2, lanes])).astype(BF16)
        all_lanes.append(lanes)
        qts.append(qt)
        dots.append(dot)
        lows.append(weights.astype(BF16))
        grads.append(grad_scores)

    def joined(parts):
        return jnp.concatenate(parts, axis=1)

    span = slice(all_lanes[0].start, all_lanes[-1].stop)
    change = tn(kv[:, :HD], joined(grads))
    if fresh:
        dqt_ref[:, span] = change
    else:
        dqt_ref[:, span] += change
    dkt = nt(joined(qts), joined(grads)) * SCALE
    dvt = nt(joined(dots), joined(lows))
    return jnp.concatenate([dkt, dvt], axis=0)


def reaches(docs_ref, key_block, row_block):
    last = docs_ref[pl.ds(key_block, 1), :][0, docs_ref.shape[1] - 1]
    return last >= docs_ref[pl.ds(row_block, 1), :][0, 0]


def blank_kernel(stats_ref):
    stats_ref[...] = jnp.zeros(stats_ref.shape, F32)
    stats_ref[0:1, :] = jnp.full((1, stats_ref.shape[1]), LOWEST, F32)


def pack_kernel(after_ref, key_ref, value_ref, kv_ref):
    kv_ref[:, :HD] = key_ref[...]
    kv_ref[:, HD:] = value_ref[...]


def turn_kernel(q_own, do_own, q_par, do_par, qd_own, qd_par):
    rows, columns = q_own.shape
    for q_ref, do_ref, qd_ref in ((q_own, do_own, qd_own), (q_par, do_par, qd_par)):
        for top, ref in ((0, q_ref), (HD, do_ref)):
            turned = jnp.transpose(ref[...])
            for head in range(columns // HD):
                qd_ref[top : top + HD, head * rows : (head + 1) * rows] = turned[
                    head * HD : (head + 1) * HD, :
                ]


def own_stats_kernel(khot_ref, rhot_ref, qd_own, qd_par, kv_ref, stats_in, stats_ref):
    chip, core = place()
    stats_ref[...] = stats_in[...]
    kv, khot, qds = kv_ref[...], khot_ref[chip], (qd_own, qd_par)
    add_stats(stats_ref, kv, khot, qds, rhot_ref, (0,), True)

    @pl.when(core == 0)
    def _():
        add_stats(stats_ref, kv, khot, qds, rhot_ref, (1,), False)


def each_remote(first, kv_ref, docs_ref, body, rest):
    chip, core = place()
    count = kv_ref.shape[0]

    def step(slot):
        source = chip ^ (first + slot)

        @pl.when(source < chip)
        def _():
            active = reaches(docs_ref, source * 2 + core, chip * 2)
            pl.when(active)(functools.partial(body, slot, source))
            if rest is not None:
                pl.when(jnp.logical_not(active))(rest)

        if rest is not None:
            pl.when(source > chip)(rest)

    if count == 1:
        step(0)
    else:
        pl.loop(0, count)(step)


def far_stats_kernel(firsts, docs_ref, khot_ref, rhot_ref, qd_own, qd_par, stats_in, *rest):
    kv_refs, stats_ref = rest[:-1], rest[-1]
    stats_ref[...] = stats_in[...]
    qds = qd_own, qd_par
    for first, kv_ref in zip(firsts, kv_refs):

        def body(slot, source, kv_ref=kv_ref):
            add_stats(stats_ref, kv_ref[slot], khot_ref[source], qds, rhot_ref, (0, 1), False)

        each_remote(first, kv_ref, docs_ref, body, None)


def norm_kernel(stats_ref, other_ref, norm_ref):
    half = stats_ref.shape[1] // 2
    mine = stats_ref[...]
    other = other_ref[...]
    other = jnp.concatenate([other[:, half:], other[:, :half]], axis=1)
    top = jnp.maximum(mine[0:1], other[0:1])
    mine_by = jnp.exp2(mine[0:1] - top)
    other_by = jnp.exp2(other[0:1] - top)
    total = mine[1:2] * mine_by + other[1:2] * other_by
    norm_ref[...] = jnp.zeros(norm_ref.shape, F32)
    norm_ref[0:1, :] = top + jnp.log2(total)
    norm_ref[1:2, :] = (mine[2:3] * mine_by + other[2:3] * other_by) / total


def far_grads_kernel(
    later, first, docs_ref, khot_ref, rhot_ref, qd_own, qd_par, norm_ref, kv_ref, *rest
):
    held = (len(rest) - later - 2) // 2
    out_ref, dqt_ref = rest[later + held : later + held + 2]
    alone = kv_ref.shape[0] == 1
    qds = qd_own, qd_par

    def clear():
        dqt_ref[...] = jnp.zeros(dqt_ref.shape, F32)
        out_ref[...] = jnp.zeros(out_ref.shape, BF16)

    if not alone:
        clear()

    def body(slot, source):
        part = add_grads(
            kv_ref[slot], khot_ref[source], qds, rhot_ref, (0, 1), False, norm_ref, dqt_ref, alone
        )
        out_ref[slot] = part.astype(BF16)

    each_remote(first, kv_ref, docs_ref, body, clear if alone else None)


def own_grads_kernel(after_ref, khot_ref, rhot_ref, qd_own, qd_par, norm_ref, kv_ref, *rest):
    dqt_in, (dkv_ref, dq_own, dq_par, dqt_ref) = rest[:-4], rest[-4:]
    rows = kv_ref.shape[0]
    heads = qd_own.shape[1] // rows
    chip, core = place()
    dqt_ref[...] = sum(part[...] for part in dqt_in)
    kv, khot, qds = kv_ref[...], khot_ref[chip], (qd_own, qd_par)
    dkv_ref[...] = add_grads(kv, khot, qds, rhot_ref, (0,), True, norm_ref, dqt_ref, False)

    @pl.when(core == 0)
    def _():
        dkv_ref[...] += add_grads(kv, khot, qds, rhot_ref, (1,), False, norm_ref, dqt_ref, False)

    for side, out_ref in enumerate((dq_own, dq_par)):
        for head in range(heads):
            chunk = side * heads + head
            out_ref[head * HD : (head + 1) * HD, :] = (
                dqt_ref[:, chunk * rows : (chunk + 1) * rows] * SCALE
            )


def query_kernel(dq_own, dq_far, dq_ref, token_ref):
    token_ref[...] = jnp.zeros(token_ref.shape, F32)
    dq_ref[...] = jnp.transpose(dq_own[...] + dq_far[...]).astype(BF16)


def hops_of(share):
    return [1, 2, 3] if share == 4 else list(range(1, share))


def next_of(share, member, away):
    line = list(range(share))
    return line[(line.index(member) + away) % share]


def combine_kernel(share, count, dq_in, own_ref, *rest):
    parts, outs = rest[:count], rest[count:]
    keep_ref, send_refs, sum_ref = outs[1], outs[2:-1], outs[-1]
    width = HD // share
    total = own_ref[...]
    for part in parts:
        total = total + part[...].astype(F32)
    sum_ref[...] = total
    member = lax.axis_index("grp") % share
    for away, out_ref in zip((0, *hops_of(share)), (keep_ref, *send_refs)):
        target = sum((member == i) * next_of(share, i, away) for i in range(share))
        first = pl.multiple_of(target * width, width)
        for half in range(2):
            piece = sum_ref[pl.ds(half * HD + first, width), :]
            out_ref[half * width : (half + 1) * width, :] = piece.astype(out_ref.dtype)


def finish_kernel(after_ref, keep_ref, *rest):
    parts, (dk_ref, dv_ref) = rest[:-2], rest[-2:]
    total = keep_ref[...]
    for part in parts:
        total = total + part[...].astype(F32)
    width = total.shape[0] // 2
    dk_ref[...] = total[:width].astype(BF16)
    dv_ref[...] = total[width:].astype(BF16)


VMEM = pl.BlockSpec(memory_space=pltpu.VMEM)
ANY = pl.BlockSpec(memory_space=pl.ANY)


HBM = pl.BlockSpec(memory_space=pltpu.HBM)


def call(kernel, out_shape, operands, scratch=(), unread=(), aliases={}, us=0, hbm=0, vmem=24):
    kinds = [HBM] * hbm + [VMEM] * (len(operands) - hbm)
    results = [VMEM] * len(out_shape)
    for place_of in unread:
        kinds[place_of] = ANY
    for source, target in aliases.items():
        kinds[source] = ANY
        results[target] = ANY
    cost = pl.CostEstimate(flops=us * 10**9, bytes_accessed=1 << 19, transcendentals=0)
    return pl.pallas_call(
        kernel,
        out_shape=out_shape,
        in_specs=kinds,
        out_specs=results,
        scratch_shapes=list(scratch),
        input_output_aliases=aliases,
        cost_estimate=cost,
        compiler_params=pltpu.CompilerParams(vmem_limit_bytes=vmem << 20),
    )(*operands)


def sds(shape, dtype):
    return jax.ShapeDtypeStruct(shape, dtype)


def on_device(queries, key_rows, value_rows, grad_output, doc_ids):
    rows, columns = queries.shape
    heads = columns // HD
    srv = lax.axis_size("srv")
    chips = srv // 2
    grp = lax.axis_size("grp")
    kv_heads = key_rows.shape[1] // HD
    share = grp // kv_heads
    lanes = 2 * heads * rows
    if kv_heads > 1:
        first = lax.axis_index("grp") // share * HD
        key_rows = lax.dynamic_slice_in_dim(key_rows, first, HD, 1)
        value_rows = lax.dynamic_slice_in_dim(value_rows, first, HD, 1)
    (blank,) = call(blank_kernel, [sds((8, lanes), F32)], [], us=5)
    (own_kv,) = call(
        pack_kernel,
        [sds((rows, 2 * HD), BF16)],
        [blank, key_rows, value_rows],
        unread=[0],
    )
    docs = doc_ids.reshape(srv, rows)

    apart = DOC_MOST.get(srv * rows, srv * rows) <= 5 * rows + 1

    def trade(block, away, back=False):
        pairs = [(i, i ^ 2 * away) for i in range(srv)]
        if srv == 8 and away == 3 and apart:
            pairs = [(b, a) for a, b in CORNER] if back else CORNER
        return lax.ppermute(block, "srv", pairs)

    def swap(block):
        return lax.ppermute(block, "srv", [(i, i ^ 1) for i in range(srv)])

    order = list(range(chips - 1, 0, -1))
    far_kv = {away: trade(own_kv, away)[None] for away in order}
    if chips > 4:
        far_kv = {1: jnp.concatenate([far_kv[away] for away in order[::-1]], axis=0)}
    qd_own, qd_par = call(
        turn_kernel,
        [sds((2 * HD, heads * rows), BF16)] * 2,
        [queries, grad_output, swap(queries), swap(grad_output)],
    )
    khot, rhot = call(
        hot_kernel,
        [sds((chips, rows, HD), BF16), sds((HD, 2 * rows), BF16)],
        [docs],
    )
    shared = [docs, khot, rhot, qd_own, qd_par]
    (stats,) = call(
        own_stats_kernel, [sds((8, lanes), F32)], [*shared[1:], own_kv, blank]
    )
    for firsts in [[first] for first in ([3, 1, 2] if chips == 4 else far_kv)]:
        if firsts:
            (stats,) = call(
                functools.partial(far_stats_kernel, firsts),
                [sds((8, lanes), F32)],
                [*shared, stats, *[far_kv[first] for first in firsts]],
            )
    (norm,) = call(norm_kernel, [sds((8, lanes), F32)], [stats, swap(stats)])
    turns = [3, 2, 1] if chips == 4 else list(far_kv)
    waits = {} if chips == 4 else {}
    starts = [3, 2, 1] if chips == 4 else list(far_kv)
    parts, dqt = {}, []
    for turn, first in enumerate(turns):
        kv = far_kv[first]
        later = dqt[-1:]
        held = [parts[one] for one in waits.get(turn, [])]
        base = len(shared) + 2
        part, dqt_part, *held = call(
            functools.partial(far_grads_kernel, len(later), first),
            [sds(kv.shape[:1] + (2 * HD, rows), BF16), sds((HD, lanes), F32)]
            + [sds(one.shape, BF16) for one in held],
            [*shared, norm, kv, *later, *held],
            unread=range(base, base + len(later)),
            aliases={base + len(later) + i: 2 + i for i in range(len(held))},
        )
        for one, passed in zip(waits.get(turn, []), held):
            parts[one] = passed
        parts[first] = part
        dqt.append(dqt_part)
    came = [
        trade(parts[first][slot], first + slot, True)
        for first in starts
        for slot in range(parts[first].shape[0])
    ]
    own_dkv, dq_own, dq_par = call(
        own_grads_kernel,
        [sds((2 * HD, rows), F32)] + [sds((columns, rows), F32)] * 2,
        [came[0], *shared[1:], norm, own_kv, *dqt],
        scratch=[pltpu.VMEM((HD, lanes), F32)],
        unread=[0],
        us=4,
    )
    width = HD // share
    dq_par, keep, *send = call(
        functools.partial(combine_kernel, share, len(came)),
        [sds(dq_par.shape, F32), sds((2 * width, rows), F32)]
        + [sds((2 * width, rows), BF16)] * (share - 1),
        [dq_par, own_dkv, *came],
        scratch=[pltpu.VMEM((2 * HD, rows), F32)],
        aliases={0: 0},
    )
    back = [
        lax.ppermute(part, "grp", [(i, i // share * share + next_of(share, i % share, away)) for i in range(grp)])
        for away, part in zip(hops_of(share), send)
    ]
    grad_query, token = call(
        query_kernel,
        [sds((rows, columns), BF16), sds((8, 128), F32)],
        [dq_own, swap(dq_par)],
        us=2,
    )
    grad_key, grad_value = call(
        finish_kernel,
        [sds((width, rows), BF16)] * 2,
        [token, keep, *back],
        unread=[0],
    )
    return grad_query, grad_key.T, grad_value.T


def solution(mesh):
    in_specs = (P("srv", "grp"), P("srv", None), P("srv", None), P("srv", "grp"), P())
    out_specs = (P("srv", "grp"), P("srv", "grp"), P("srv", "grp"))
    return jax.shard_map(
        on_device, mesh=mesh, in_specs=in_specs, out_specs=out_specs, check_vma=False
    )
```

```python
import functools

import jax
import jax.numpy as jnp
from jax import lax
from jax.experimental import pallas as pl
from jax.experimental.pallas import tpu as pltpu
from jax.sharding import PartitionSpec as P

HD = 128
SCALE = HD**-0.5
LOG2E = 1.4426950408889634
MASKED = -1.0e30
LOWEST = -1.0e20
DOC_MOST = {2048: 1280, 8192: 4352}
CORNER = [(1, 7), (7, 6), (6, 2), (2, 4), (4, 0), (0, 1), (3, 5), (5, 3)]
F32 = jnp.float32
BF16 = jnp.bfloat16


def nn(a, b):
    return lax.dot_general(a, b, (((1,), (0,)), ((), ())), preferred_element_type=F32)


def nt(a, b):
    return lax.dot_general(a, b, (((1,), (1,)), ((), ())), preferred_element_type=F32)


def tn(a, b):
    return lax.dot_general(a, b, (((0,), (0,)), ((), ())), preferred_element_type=F32)


def place():
    srv = lax.axis_index("srv")
    return srv // 2, srv % 2


def hot_kernel(docs_ref, khot_ref, rhot_ref):
    rows = docs_ref.shape[1]
    chip, core = place()
    kind = lax.broadcasted_iota(jnp.int32, (HD, rows), 0)
    for source in range(khot_ref.shape[0]):
        hot = kind == docs_ref[pl.ds(source * 2 + core, 1), :]
        khot_ref[source] = jnp.transpose(hot.astype(F32)).astype(BF16)
    for side in range(2):
        row_block = chip * 2 + (core if side == 0 else 1 - core)
        hot = kind == docs_ref[pl.ds(row_block, 1), :]
        rhot_ref[:, side * rows : (side + 1) * rows] = jnp.where(hot, 0.0, MASKED).astype(BF16)


def chunks_of(sides, qds, rhot_ref):
    rows = rhot_ref.shape[1] // 2
    heads = qds[0].shape[1] // rows
    for side in sides:
        for head in range(heads):
            local = slice(head * rows, (head + 1) * rows)
            chunk = side * heads + head
            lanes = slice(chunk * rows, (chunk + 1) * rows)
            penalty = rhot_ref[:, side * rows : (side + 1) * rows]
            yield lanes, qds[side][:HD, local], qds[side][HD:, local], penalty


def scores_of(kv, khot, qt, penalty, causal):
    keys = jnp.concatenate([kv[:, :HD], khot], axis=1)
    scores = nn(keys, jnp.concatenate([qt, penalty], axis=0))
    if causal:
        key_pos = lax.broadcasted_iota(jnp.int32, scores.shape, 0)
        row_pos = lax.broadcasted_iota(jnp.int32, scores.shape, 1)
        scores = jnp.where(key_pos <= row_pos, scores, MASKED)
    return scores


def add_stats(stats_ref, kv, khot, qds, rhot_ref, sides, causal, keep=()):
    for lanes, qt, dot, penalty in chunks_of(sides, qds, rhot_ref):
        scores = scores_of(kv, khot, qt, penalty, causal)
        grad_probs = nn(kv[:, HD:], dot)
        old = stats_ref[0:1, lanes]
        new = jnp.maximum(old, jnp.max(scores, axis=0, keepdims=True) * (SCALE * LOG2E))
        factor = jnp.exp2(old - new)
        weights = jnp.exp2(scores * (SCALE * LOG2E) - new)
        for ref, kept in zip(keep, (weights, grad_probs)):
            ref[:, lanes] = kept
        stats_ref[0:1, lanes] = new
        stats_ref[1:2, lanes] = stats_ref[1:2, lanes] * factor + jnp.sum(
            weights, axis=0, keepdims=True
        )
        stats_ref[2:3, lanes] = stats_ref[2:3, lanes] * factor + jnp.sum(
            weights * grad_probs, axis=0, keepdims=True
        )


def add_grads(kv, khot, qds, rhot_ref, sides, causal, norm_ref, dqt_ref, fresh, keep=()):
    qts, dots, lows, grads, all_lanes = [], [], [], [], []
    for lanes, qt, dot, penalty in chunks_of(sides, qds, rhot_ref):
        if keep:
            top_ref, weights_ref, probs_ref = keep
            factor = jnp.exp2(top_ref[0:1, lanes] - norm_ref[0:1, lanes])
            weights = weights_ref[:, lanes] * factor
            grad_probs = probs_ref[:, lanes]
        else:
            scores = scores_of(kv, khot, qt, penalty, causal)
            weights = jnp.exp2(scores * (SCALE * LOG2E) - norm_ref[0:1, lanes])
            grad_probs = nn(kv[:, HD:], dot)
        grad_scores = (weights * (grad_probs - norm_ref[1:2, lanes])).astype(BF16)
        all_lanes.append(lanes)
        qts.append(qt)
        dots.append(dot)
        lows.append(weights.astype(BF16))
        grads.append(grad_scores)

    def joined(parts):
        return jnp.concatenate(parts, axis=1)

    span = slice(all_lanes[0].start, all_lanes[-1].stop)
    change = tn(kv[:, :HD], joined(grads))
    if fresh:
        dqt_ref[:, span] = change
    else:
        dqt_ref[:, span] += change
    dkt = nt(joined(qts), joined(grads)) * SCALE
    dvt = nt(joined(dots), joined(lows))
    return jnp.concatenate([dkt, dvt], axis=0)


def reaches(docs_ref, key_block, row_block):
    last = docs_ref[pl.ds(key_block, 1), :][0, docs_ref.shape[1] - 1]
    return last >= docs_ref[pl.ds(row_block, 1), :][0, 0]


def blank_kernel(stats_ref):
    stats_ref[...] = jnp.zeros(stats_ref.shape, F32)
    stats_ref[0:1, :] = jnp.full((1, stats_ref.shape[1]), LOWEST, F32)


def pack_kernel(after_ref, key_ref, value_ref, kv_ref):
    kv_ref[:, :HD] = key_ref[...]
    kv_ref[:, HD:] = value_ref[...]


def turn_kernel(q_own, do_own, q_par, do_par, qd_own, qd_par):
    rows, columns = q_own.shape
    for q_ref, do_ref, qd_ref in ((q_own, do_own, qd_own), (q_par, do_par, qd_par)):
        for top, ref in ((0, q_ref), (HD, do_ref)):
            turned = jnp.transpose(ref[...])
            for head in range(columns // HD):
                qd_ref[top : top + HD, head * rows : (head + 1) * rows] = turned[
                    head * HD : (head + 1) * HD, :
                ]


def own_stats_kernel(khot_ref, rhot_ref, qd_own, qd_par, kv_ref, stats_in, stats_ref):
    chip, core = place()
    stats_ref[...] = stats_in[...]
    kv, khot, qds = kv_ref[...], khot_ref[chip], (qd_own, qd_par)
    add_stats(stats_ref, kv, khot, qds, rhot_ref, (0,), True)

    @pl.when(core == 0)
    def _():
        add_stats(stats_ref, kv, khot, qds, rhot_ref, (1,), False)


def each_remote(first, kv_ref, docs_ref, body, rest):
    chip, core = place()
    count = kv_ref.shape[0]

    def step(slot):
        source = chip ^ (first + slot)

        @pl.when(source < chip)
        def _():
            active = reaches(docs_ref, source * 2 + core, chip * 2)
            pl.when(active)(functools.partial(body, slot, source))
            if rest is not None:
                pl.when(jnp.logical_not(active))(rest)

        if rest is not None:
            pl.when(source > chip)(rest)

    if count == 1:
        step(0)
    else:
        pl.loop(0, count)(step)


def far_stats_kernel(first, docs_ref, khot_ref, rhot_ref, qd_own, qd_par, stats_in, kv_ref, *outs):
    stats_ref, keep = outs[0], outs[1:]
    stats_ref[...] = stats_in[...]
    qds = qd_own, qd_par

    def body(slot, source):
        add_stats(stats_ref, kv_ref[slot], khot_ref[source], qds, rhot_ref, (0, 1), False, keep)

    each_remote(first, kv_ref, docs_ref, body, None)


def norm_kernel(stats_ref, other_ref, norm_ref):
    half = stats_ref.shape[1] // 2
    mine = stats_ref[...]
    other = other_ref[...]
    other = jnp.concatenate([other[:, half:], other[:, :half]], axis=1)
    top = jnp.maximum(mine[0:1], other[0:1])
    mine_by = jnp.exp2(mine[0:1] - top)
    other_by = jnp.exp2(other[0:1] - top)
    total = mine[1:2] * mine_by + other[1:2] * other_by
    norm_ref[...] = jnp.zeros(norm_ref.shape, F32)
    norm_ref[0:1, :] = top + jnp.log2(total)
    norm_ref[1:2, :] = (mine[2:3] * mine_by + other[2:3] * other_by) / total


def far_grads_kernel(
    first, docs_ref, khot_ref, rhot_ref, qd_own, qd_par, norm_ref, kv_ref, before_ref, *rest
):
    keep, (out_ref, dqt_ref) = rest[:-2], rest[-2:]
    alone = kv_ref.shape[0] == 1
    qds = qd_own, qd_par

    def clear():
        dqt_ref[...] = jnp.zeros(dqt_ref.shape, F32)
        out_ref[...] = jnp.zeros(out_ref.shape, BF16)

    if not alone:
        clear()

    def body(slot, source):
        kv, khot = kv_ref[slot], khot_ref[source]
        part = add_grads(
            kv, khot, qds, rhot_ref, (0, 1), False, norm_ref, dqt_ref, alone, keep
        )
        out_ref[slot] = part.astype(BF16)

    each_remote(first, kv_ref, docs_ref, body, clear if alone else None)


def own_grads_kernel(khot_ref, rhot_ref, qd_own, qd_par, norm_ref, kv_ref, *rest):
    dqt_in, (dkv_ref, dq_own, dq_par, dqt_ref) = rest[:-4], rest[-4:]
    rows = kv_ref.shape[0]
    heads = qd_own.shape[1] // rows
    chip, core = place()
    dqt_ref[...] = sum(part[...] for part in dqt_in)
    kv, khot, qds = kv_ref[...], khot_ref[chip], (qd_own, qd_par)
    dkv_ref[...] = add_grads(kv, khot, qds, rhot_ref, (0,), True, norm_ref, dqt_ref, False)

    @pl.when(core == 0)
    def _():
        dkv_ref[...] += add_grads(kv, khot, qds, rhot_ref, (1,), False, norm_ref, dqt_ref, False)

    for side, out_ref in enumerate((dq_own, dq_par)):
        for head in range(heads):
            chunk = side * heads + head
            out_ref[head * HD : (head + 1) * HD, :] = (
                dqt_ref[:, chunk * rows : (chunk + 1) * rows] * SCALE
            )


def query_kernel(dq_own, dq_far, dq_ref, token_ref):
    token_ref[...] = jnp.zeros(token_ref.shape, F32)
    dq_ref[...] = jnp.transpose(dq_own[...] + dq_far[...]).astype(BF16)


def hops_of(share):
    return [1, 2, 3] if share == 4 else list(range(1, share))


def next_of(share, member, away):
    line = list(range(share))
    return line[(line.index(member) + away) % share]


def combine_kernel(share, count, dq_in, own_ref, *rest):
    parts, outs = rest[:count], rest[count:]
    keep_ref, send_refs, sum_ref = outs[1], outs[2:-1], outs[-1]
    width = HD // share
    total = own_ref[...]
    for part in parts:
        total = total + part[...].astype(F32)
    sum_ref[...] = total
    member = lax.axis_index("grp") % share
    for away, out_ref in zip((0, *hops_of(share)), (keep_ref, *send_refs)):
        target = sum((member == i) * next_of(share, i, away) for i in range(share))
        first = pl.multiple_of(target * width, width)
        for half in range(2):
            piece = sum_ref[pl.ds(half * HD + first, width), :]
            out_ref[half * width : (half + 1) * width, :] = piece.astype(out_ref.dtype)


def finish_kernel(after_ref, keep_ref, *rest):
    parts, (dk_ref, dv_ref) = rest[:-2], rest[-2:]
    total = keep_ref[...]
    for part in parts:
        total = total + part[...].astype(F32)
    width = total.shape[0] // 2
    dk_ref[...] = total[:width].astype(BF16)
    dv_ref[...] = total[width:].astype(BF16)


VMEM = pl.BlockSpec(memory_space=pltpu.VMEM)
ANY = pl.BlockSpec(memory_space=pl.ANY)


HBM = pl.BlockSpec(memory_space=pltpu.HBM)


def call(kernel, out_shape, operands, scratch=(), unread=(), aliases={}, us=0, hbm=0, vmem=24):
    kinds = [HBM] * hbm + [VMEM] * (len(operands) - hbm)
    results = [VMEM] * len(out_shape)
    for place_of in unread:
        kinds[place_of] = ANY
    for source, target in aliases.items():
        kinds[source] = ANY
        results[target] = ANY
    cost = pl.CostEstimate(flops=us * 10**9, bytes_accessed=1 << 19, transcendentals=0)
    return pl.pallas_call(
        kernel,
        out_shape=out_shape,
        in_specs=kinds,
        out_specs=results,
        scratch_shapes=list(scratch),
        input_output_aliases=aliases,
        cost_estimate=cost,
        compiler_params=pltpu.CompilerParams(vmem_limit_bytes=vmem << 20),
    )(*operands)


def sds(shape, dtype):
    return jax.ShapeDtypeStruct(shape, dtype)


def on_device(queries, key_rows, value_rows, grad_output, doc_ids):
    rows, columns = queries.shape
    heads = columns // HD
    srv = lax.axis_size("srv")
    chips = srv // 2
    grp = lax.axis_size("grp")
    kv_heads = key_rows.shape[1] // HD
    share = grp // kv_heads
    lanes = 2 * heads * rows
    if kv_heads > 1:
        first = lax.axis_index("grp") // share * HD
        key_rows = lax.dynamic_slice_in_dim(key_rows, first, HD, 1)
        value_rows = lax.dynamic_slice_in_dim(value_rows, first, HD, 1)
    (blank,) = call(blank_kernel, [sds((8, lanes), F32)], [], us=5)
    (own_kv,) = call(
        pack_kernel,
        [sds((rows, 2 * HD), BF16)],
        [blank, key_rows, value_rows],
        unread=[0],
    )
    docs = doc_ids.reshape(srv, rows)

    apart = DOC_MOST.get(srv * rows, srv * rows) <= 5 * rows + 1

    def trade(block, away, back=False):
        pairs = [(i, i ^ 2 * away) for i in range(srv)]
        if srv == 8 and away == 3 and apart:
            pairs = [(4, 2), (5, 3), (7, 1), (6, 5), (0, 4), (1, 0), (2, 6), (3, 7)] if back else CORNER
        return lax.ppermute(block, "srv", pairs)

    def swap(block):
        return lax.ppermute(block, "srv", [(i, i ^ 1) for i in range(srv)])

    order = list(range(chips - 1, 0, -1))
    far_kv = {away: trade(own_kv, away)[None] for away in order}
    if chips > 4:
        far_kv = {1: jnp.concatenate([far_kv[away] for away in order[::-1]], axis=0)}
    qd_own, qd_par = call(
        turn_kernel,
        [sds((2 * HD, heads * rows), BF16)] * 2,
        [queries, grad_output, swap(queries), swap(grad_output)],
    )
    khot, rhot = call(
        hot_kernel,
        [sds((chips, rows, HD), BF16), sds((HD, 2 * rows), BF16)],
        [docs],
    )
    shared = [docs, khot, rhot, qd_own, qd_par]
    (stats,) = call(
        own_stats_kernel, [sds((8, lanes), F32)], [*shared[1:], own_kv, blank]
    )
    turns = [3, 1, 2] if chips == 4 else list(far_kv)
    kept = {}
    for first in turns:
        saved = [sds((rows, lanes), F32)] * 2 if chips == 4 else []
        stats, *saved = call(
            functools.partial(far_stats_kernel, first),
            [sds((8, lanes), F32)] + saved,
            [*shared, stats, far_kv[first]],
        )
        kept[first] = [stats, *saved] if saved else []
    (norm,) = call(norm_kernel, [sds((8, lanes), F32)], [stats, swap(stats)])
    parts, dqt = {}, [norm]
    turns = [3, 2, 1] if chips == 4 else turns
    for first in turns:
        kv = far_kv[first]
        parts[first], dqt_part = call(
            functools.partial(far_grads_kernel, first),
            [sds(kv.shape[:1] + (2 * HD, rows), BF16), sds((HD, lanes), F32)],
            [*shared, norm, kv, dqt[-1], *kept[first]],
            unread=[len(shared) + 2],
        )
        dqt.append(dqt_part)
    came = [
        trade(parts[first][slot], first + slot, True)
        for first in turns
        for slot in range(parts[first].shape[0])
    ]
    own_dkv, dq_own, dq_par = call(
        own_grads_kernel,
        [sds((2 * HD, rows), F32)] + [sds((columns, rows), F32)] * 2,
        [*shared[1:], norm, own_kv, *dqt[1:]],
        scratch=[pltpu.VMEM((HD, lanes), F32)],
        us=4,
    )
    width = HD // share
    dq_par, keep, *send = call(
        functools.partial(combine_kernel, share, len(came)),
        [sds(dq_par.shape, F32), sds((2 * width, rows), F32)]
        + [sds((2 * width, rows), BF16)] * (share - 1),
        [dq_par, own_dkv, *came],
        scratch=[pltpu.VMEM((2 * HD, rows), F32)],
        aliases={0: 0},
    )
    back = [
        lax.ppermute(part, "grp", [(i, i // share * share + next_of(share, i % share, away)) for i in range(grp)])
        for away, part in zip(hops_of(share), send)
    ]
    grad_query, token = call(
        query_kernel,
        [sds((rows, columns), BF16), sds((8, 128), F32)],
        [dq_own, swap(dq_par)],
        us=2,
    )
    grad_key, grad_value = call(
        finish_kernel,
        [sds((width, rows), BF16)] * 2,
        [token, keep, *back],
        unread=[0],
    )
    return grad_query, grad_key.T, grad_value.T


def solution(mesh):
    in_specs = (P("srv", "grp"), P("srv", None), P("srv", None), P("srv", "grp"), P())
    out_specs = (P("srv", "grp"), P("srv", "grp"), P("srv", "grp"))
    return jax.shard_map(
        on_device, mesh=mesh, in_specs=in_specs, out_specs=out_specs, check_vma=False
    )
```

```python
import functools

import jax
import jax.numpy as jnp
from jax import lax
from jax.experimental import pallas as pl
from jax.experimental.pallas import tpu as pltpu
from jax.sharding import PartitionSpec as P

HD = 128
SCALE = HD**-0.5
LOG2E = 1.4426950408889634
MASKED = -1.0e30
LOWEST = -1.0e20
DOC_MOST = {2048: 1280, 8192: 4352}
CORNER = [(1, 7), (7, 6), (6, 2), (2, 4), (4, 0), (0, 1), (3, 5), (5, 3)]
F32 = jnp.float32
BF16 = jnp.bfloat16


def nn(a, b):
    return lax.dot_general(a, b, (((1,), (0,)), ((), ())), preferred_element_type=F32)


def nt(a, b):
    return lax.dot_general(a, b, (((1,), (1,)), ((), ())), preferred_element_type=F32)


def tn(a, b):
    return lax.dot_general(a, b, (((0,), (0,)), ((), ())), preferred_element_type=F32)


def place():
    srv = lax.axis_index("srv")
    return srv // 2, srv % 2


def hot_kernel(docs_ref, khot_ref, rhot_ref):
    rows = docs_ref.shape[1]
    chip, core = place()
    kind = lax.broadcasted_iota(jnp.int32, (HD, rows), 0)
    for source in range(khot_ref.shape[0]):
        hot = kind == docs_ref[pl.ds(source * 2 + core, 1), :]
        khot_ref[source] = jnp.transpose(hot.astype(F32)).astype(BF16)
    for side in range(2):
        row_block = chip * 2 + (core if side == 0 else 1 - core)
        hot = kind == docs_ref[pl.ds(row_block, 1), :]
        rhot_ref[:, side * rows : (side + 1) * rows] = jnp.where(hot, 0.0, MASKED).astype(BF16)


def chunks_of(sides, qds, rhot_ref):
    rows = rhot_ref.shape[1] // 2
    heads = qds[0].shape[1] // rows
    for side in sides:
        for head in range(heads):
            local = slice(head * rows, (head + 1) * rows)
            chunk = side * heads + head
            lanes = slice(chunk * rows, (chunk + 1) * rows)
            penalty = rhot_ref[:, side * rows : (side + 1) * rows]
            yield lanes, qds[side][:HD, local], qds[side][HD:, local], penalty


def scores_of(kv, khot, qt, penalty, causal):
    keys = jnp.concatenate([kv[:, :HD], khot], axis=1)
    scores = nn(keys, jnp.concatenate([qt, penalty], axis=0))
    if causal:
        key_pos = lax.broadcasted_iota(jnp.int32, scores.shape, 0)
        row_pos = lax.broadcasted_iota(jnp.int32, scores.shape, 1)
        scores = jnp.where(key_pos <= row_pos, scores, MASKED)
    return scores


def add_stats(stats_ref, kv, khot, qds, rhot_ref, sides, causal, keep=()):
    for lanes, qt, dot, penalty in chunks_of(sides, qds, rhot_ref):
        scores = scores_of(kv, khot, qt, penalty, causal)
        grad_probs = nn(kv[:, HD:], dot)
        old = stats_ref[0:1, lanes]
        new = jnp.maximum(old, jnp.max(scores, axis=0, keepdims=True) * (SCALE * LOG2E))
        factor = jnp.exp2(old - new)
        weights = jnp.exp2(scores * (SCALE * LOG2E) - new)
        for ref, kept in zip(keep, (weights, grad_probs)):
            ref[:, lanes] = kept
        stats_ref[0:1, lanes] = new
        stats_ref[1:2, lanes] = stats_ref[1:2, lanes] * factor + jnp.sum(
            weights, axis=0, keepdims=True
        )
        stats_ref[2:3, lanes] = stats_ref[2:3, lanes] * factor + jnp.sum(
            weights * grad_probs, axis=0, keepdims=True
        )


def add_grads(kv, khot, qds, rhot_ref, sides, causal, norm_ref, dqt_ref, fresh, keep=()):
    qts, dots, lows, grads, all_lanes = [], [], [], [], []
    for lanes, qt, dot, penalty in chunks_of(sides, qds, rhot_ref):
        if keep:
            top_ref, weights_ref, probs_ref = keep
            factor = jnp.exp2(top_ref[0:1, lanes] - norm_ref[0:1, lanes])
            weights = weights_ref[:, lanes] * factor
            grad_probs = probs_ref[:, lanes]
        else:
            scores = scores_of(kv, khot, qt, penalty, causal)
            weights = jnp.exp2(scores * (SCALE * LOG2E) - norm_ref[0:1, lanes])
            grad_probs = nn(kv[:, HD:], dot)
        grad_scores = (weights * (grad_probs - norm_ref[1:2, lanes])).astype(BF16)
        all_lanes.append(lanes)
        qts.append(qt)
        dots.append(dot)
        lows.append(weights.astype(BF16))
        grads.append(grad_scores)

    def joined(parts):
        return jnp.concatenate(parts, axis=1)

    span = slice(all_lanes[0].start, all_lanes[-1].stop)
    change = tn(kv[:, :HD], joined(grads))
    if fresh:
        dqt_ref[:, span] = change
    else:
        dqt_ref[:, span] += change
    dkt = nt(joined(qts), joined(grads)) * SCALE
    dvt = nt(joined(dots), joined(lows))
    return jnp.concatenate([dkt, dvt], axis=0)


def reaches(docs_ref, key_block, row_block):
    last = docs_ref[pl.ds(key_block, 1), :][0, docs_ref.shape[1] - 1]
    return last >= docs_ref[pl.ds(row_block, 1), :][0, 0]


def blank_kernel(stats_ref):
    stats_ref[...] = jnp.zeros(stats_ref.shape, F32)
    stats_ref[0:1, :] = jnp.full((1, stats_ref.shape[1]), LOWEST, F32)


def pack_kernel(after_ref, key_ref, value_ref, kv_ref):
    kv_ref[:, :HD] = key_ref[...]
    kv_ref[:, HD:] = value_ref[...]


def turn_kernel(q_own, do_own, q_par, do_par, qd_own, qd_par):
    rows, columns = q_own.shape
    for q_ref, do_ref, qd_ref in ((q_own, do_own, qd_own), (q_par, do_par, qd_par)):
        for top, ref in ((0, q_ref), (HD, do_ref)):
            turned = jnp.transpose(ref[...])
            for head in range(columns // HD):
                qd_ref[top : top + HD, head * rows : (head + 1) * rows] = turned[
                    head * HD : (head + 1) * HD, :
                ]


def own_stats_kernel(khot_ref, rhot_ref, qd_own, qd_par, kv_ref, stats_in, stats_ref):
    chip, core = place()
    stats_ref[...] = stats_in[...]
    kv, khot, qds = kv_ref[...], khot_ref[chip], (qd_own, qd_par)
    add_stats(stats_ref, kv, khot, qds, rhot_ref, (0,), True)

    @pl.when(core == 0)
    def _():
        add_stats(stats_ref, kv, khot, qds, rhot_ref, (1,), False)


def each_remote(first, kv_ref, docs_ref, body, rest):
    chip, core = place()
    count = kv_ref.shape[0]

    def step(slot):
        source = chip ^ (first + slot)

        @pl.when(source < chip)
        def _():
            active = reaches(docs_ref, source * 2 + core, chip * 2)
            pl.when(active)(functools.partial(body, slot, source))
            if rest is not None:
                pl.when(jnp.logical_not(active))(rest)

        if rest is not None:
            pl.when(source > chip)(rest)

    if count == 1:
        step(0)
    else:
        pl.loop(0, count)(step)


def far_stats_kernel(first, docs_ref, khot_ref, rhot_ref, qd_own, qd_par, stats_in, kv_ref, *outs):
    stats_ref, keep = outs[0], outs[1:]
    stats_ref[...] = stats_in[...]
    qds = qd_own, qd_par

    def body(slot, source):
        add_stats(stats_ref, kv_ref[slot], khot_ref[source], qds, rhot_ref, (0, 1), False, keep)

    each_remote(first, kv_ref, docs_ref, body, None)


def norm_kernel(stats_ref, other_ref, norm_ref):
    half = stats_ref.shape[1] // 2
    mine = stats_ref[...]
    other = other_ref[...]
    other = jnp.concatenate([other[:, half:], other[:, :half]], axis=1)
    top = jnp.maximum(mine[0:1], other[0:1])
    mine_by = jnp.exp2(mine[0:1] - top)
    other_by = jnp.exp2(other[0:1] - top)
    total = mine[1:2] * mine_by + other[1:2] * other_by
    norm_ref[...] = jnp.zeros(norm_ref.shape, F32)
    norm_ref[0:1, :] = top + jnp.log2(total)
    norm_ref[1:2, :] = (mine[2:3] * mine_by + other[2:3] * other_by) / total


def far_grads_kernel(
    first, docs_ref, khot_ref, rhot_ref, qd_own, qd_par, norm_ref, kv_ref, before_ref, *rest
):
    keep, (out_ref, dqt_ref) = rest[:-2], rest[-2:]
    alone = kv_ref.shape[0] == 1
    qds = qd_own, qd_par

    def clear():
        dqt_ref[...] = jnp.zeros(dqt_ref.shape, F32)
        out_ref[...] = jnp.zeros(out_ref.shape, BF16)

    if not alone:
        clear()

    def body(slot, source):
        kv, khot = kv_ref[slot], khot_ref[source]
        part = add_grads(
            kv, khot, qds, rhot_ref, (0, 1), False, norm_ref, dqt_ref, alone, keep
        )
        out_ref[slot] = part.astype(BF16)

    each_remote(first, kv_ref, docs_ref, body, clear if alone else None)


def own_grads_kernel(khot_ref, rhot_ref, qd_own, qd_par, norm_ref, kv_ref, *rest):
    dqt_in, (dkv_ref, dq_own, dq_par, dqt_ref) = rest[:-4], rest[-4:]
    rows = kv_ref.shape[0]
    heads = qd_own.shape[1] // rows
    chip, core = place()
    dqt_ref[...] = sum(part[...] for part in dqt_in)
    kv, khot, qds = kv_ref[...], khot_ref[chip], (qd_own, qd_par)
    dkv_ref[...] = add_grads(kv, khot, qds, rhot_ref, (0,), True, norm_ref, dqt_ref, False)

    @pl.when(core == 0)
    def _():
        dkv_ref[...] += add_grads(kv, khot, qds, rhot_ref, (1,), False, norm_ref, dqt_ref, False)

    for side, out_ref in enumerate((dq_own, dq_par)):
        for head in range(heads):
            chunk = side * heads + head
            out_ref[head * HD : (head + 1) * HD, :] = (
                dqt_ref[:, chunk * rows : (chunk + 1) * rows] * SCALE
            )


def query_kernel(dq_own, dq_far, dq_ref, token_ref):
    token_ref[...] = jnp.zeros(token_ref.shape, F32)
    dq_ref[...] = jnp.transpose(dq_own[...] + dq_far[...]).astype(BF16)


def hops_of(share):
    return [1, 2, 3] if share == 4 else list(range(1, share))


def next_of(share, member, away):
    line = [i ^ i >> 1 for i in range(share)]
    return line[(line.index(member) + away) % share]


def combine_kernel(share, count, dq_in, own_ref, *rest):
    parts, outs = rest[:count], rest[count:]
    keep_ref, send_refs, sum_ref = outs[1], outs[2:-1], outs[-1]
    width = HD // share
    total = own_ref[...]
    for part in parts:
        total = total + part[...].astype(F32)
    sum_ref[...] = total
    member = lax.axis_index("grp") % share
    for away, out_ref in zip((0, *hops_of(share)), (keep_ref, *send_refs)):
        target = sum((member == i) * next_of(share, i, away) for i in range(share))
        first = pl.multiple_of(target * width, width)
        for half in range(2):
            piece = sum_ref[pl.ds(half * HD + first, width), :]
            out_ref[half * width : (half + 1) * width, :] = piece.astype(out_ref.dtype)


def finish_kernel(after_ref, keep_ref, *rest):
    parts, (dk_ref, dv_ref) = rest[:-2], rest[-2:]
    total = keep_ref[...]
    for part in parts:
        total = total + part[...].astype(F32)
    width = total.shape[0] // 2
    dk_ref[...] = total[:width].astype(BF16)
    dv_ref[...] = total[width:].astype(BF16)


VMEM = pl.BlockSpec(memory_space=pltpu.VMEM)
ANY = pl.BlockSpec(memory_space=pl.ANY)


HBM = pl.BlockSpec(memory_space=pltpu.HBM)


def call(kernel, out_shape, operands, scratch=(), unread=(), aliases={}, us=0, hbm=0, vmem=24):
    kinds = [HBM] * hbm + [VMEM] * (len(operands) - hbm)
    results = [VMEM] * len(out_shape)
    for place_of in unread:
        kinds[place_of] = ANY
    for source, target in aliases.items():
        kinds[source] = ANY
        results[target] = ANY
    cost = pl.CostEstimate(flops=us * 10**9, bytes_accessed=1 << 19, transcendentals=0)
    return pl.pallas_call(
        kernel,
        out_shape=out_shape,
        in_specs=kinds,
        out_specs=results,
        scratch_shapes=list(scratch),
        input_output_aliases=aliases,
        cost_estimate=cost,
        compiler_params=pltpu.CompilerParams(vmem_limit_bytes=vmem << 20),
    )(*operands)


def sds(shape, dtype):
    return jax.ShapeDtypeStruct(shape, dtype)


def on_device(queries, key_rows, value_rows, grad_output, doc_ids):
    rows, columns = queries.shape
    heads = columns // HD
    srv = lax.axis_size("srv")
    chips = srv // 2
    grp = lax.axis_size("grp")
    kv_heads = key_rows.shape[1] // HD
    share = grp // kv_heads
    lanes = 2 * heads * rows
    if kv_heads > 1:
        first = lax.axis_index("grp") // share * HD
        key_rows = lax.dynamic_slice_in_dim(key_rows, first, HD, 1)
        value_rows = lax.dynamic_slice_in_dim(value_rows, first, HD, 1)
    (blank,) = call(blank_kernel, [sds((8, lanes), F32)], [], us=5)
    (own_kv,) = call(
        pack_kernel,
        [sds((rows, 2 * HD), BF16)],
        [blank, key_rows, value_rows],
        unread=[0],
    )
    docs = doc_ids.reshape(srv, rows)

    apart = DOC_MOST.get(srv * rows, srv * rows) <= 5 * rows + 1

    def trade(block, away, back=False):
        pairs = [(i, i ^ 2 * away) for i in range(srv)]
        if srv == 8 and away == 3 and apart:
            pairs = [(4, 2), (5, 3), (7, 1), (6, 5), (0, 4), (1, 0), (2, 6), (3, 7)] if back else CORNER
        return lax.ppermute(block, "srv", pairs)

    def swap(block):
        return lax.ppermute(block, "srv", [(i, i ^ 1) for i in range(srv)])

    order = list(range(chips - 1, 0, -1))
    far_kv = {away: trade(own_kv, away)[None] for away in order}
    if chips > 4:
        far_kv = {1: jnp.concatenate([far_kv[away] for away in order[::-1]], axis=0)}
    qd_own, qd_par = call(
        turn_kernel,
        [sds((2 * HD, heads * rows), BF16)] * 2,
        [queries, grad_output, swap(queries), swap(grad_output)],
    )
    khot, rhot = call(
        hot_kernel,
        [sds((chips, rows, HD), BF16), sds((HD, 2 * rows), BF16)],
        [docs],
    )
    shared = [docs, khot, rhot, qd_own, qd_par]
    (stats,) = call(
        own_stats_kernel, [sds((8, lanes), F32)], [*shared[1:], own_kv, blank]
    )
    turns = [3, 1, 2] if chips == 4 else list(far_kv)
    kept = {}
    for first in turns:
        saved = [sds((rows, lanes), F32)] * 2 if chips == 4 else []
        stats, *saved = call(
            functools.partial(far_stats_kernel, first),
            [sds((8, lanes), F32)] + saved,
            [*shared, stats, far_kv[first]],
        )
        kept[first] = [stats, *saved] if saved else []
    (norm,) = call(norm_kernel, [sds((8, lanes), F32)], [stats, swap(stats)])
    parts, dqt = {}, [norm]
    turns = [3, 2, 1] if chips == 4 else turns
    for first in turns:
        kv = far_kv[first]
        parts[first], dqt_part = call(
            functools.partial(far_grads_kernel, first),
            [sds(kv.shape[:1] + (2 * HD, rows), BF16), sds((HD, lanes), F32)],
            [*shared, norm, kv, dqt[-1], *kept[first]],
            unread=[len(shared) + 2],
        )
        dqt.append(dqt_part)
    came = [
        trade(parts[first][slot], first + slot, True)
        for first in turns
        for slot in range(parts[first].shape[0])
    ]
    own_dkv, dq_own, dq_par = call(
        own_grads_kernel,
        [sds((2 * HD, rows), F32)] + [sds((columns, rows), F32)] * 2,
        [*shared[1:], norm, own_kv, *dqt[1:]],
        scratch=[pltpu.VMEM((HD, lanes), F32)],
        us=4,
    )
    width = HD // share
    dq_par, keep, *send = call(
        functools.partial(combine_kernel, share, len(came)),
        [sds(dq_par.shape, F32), sds((2 * width, rows), F32)]
        + [sds((2 * width, rows), BF16)] * (share - 1),
        [dq_par, own_dkv, *came],
        scratch=[pltpu.VMEM((2 * HD, rows), F32)],
        aliases={0: 0},
    )
    back = [
        lax.ppermute(part, "grp", [(i, i // share * share + next_of(share, i % share, away)) for i in range(grp)])
        for away, part in zip(hops_of(share), send)
    ]
    grad_query, token = call(
        query_kernel,
        [sds((rows, columns), BF16), sds((8, 128), F32)],
        [dq_own, swap(dq_par)],
        us=2,
    )
    grad_key, grad_value = call(
        finish_kernel,
        [sds((width, rows), BF16)] * 2,
        [token, keep, *back],
        unread=[0],
    )
    return grad_query, grad_key.T, grad_value.T


def solution(mesh):
    in_specs = (P("srv", "grp"), P("srv", None), P("srv", None), P("srv", "grp"), P())
    out_specs = (P("srv", "grp"), P("srv", "grp"), P("srv", "grp"))
    return jax.shard_map(
        on_device, mesh=mesh, in_specs=in_specs, out_specs=out_specs, check_vma=False
    )
```

```python
import functools

import jax
import jax.numpy as jnp
from jax import lax
from jax.experimental import pallas as pl
from jax.experimental.pallas import tpu as pltpu
from jax.sharding import PartitionSpec as P

HD = 128
SCALE = HD**-0.5
LOG2E = 1.4426950408889634
MASKED = -1.0e30
LOWEST = -1.0e20
DOC_MOST = {2048: 1280, 8192: 4352}
CORNER = [(1, 7), (7, 6), (6, 2), (2, 4), (4, 0), (0, 1), (3, 5), (5, 3)]
F32 = jnp.float32
BF16 = jnp.bfloat16


def nn(a, b):
    return lax.dot_general(a, b, (((1,), (0,)), ((), ())), preferred_element_type=F32)


def nt(a, b):
    return lax.dot_general(a, b, (((1,), (1,)), ((), ())), preferred_element_type=F32)


def tn(a, b):
    return lax.dot_general(a, b, (((0,), (0,)), ((), ())), preferred_element_type=F32)


def place():
    srv = lax.axis_index("srv")
    return srv // 2, srv % 2


def hot_kernel(docs_ref, khot_ref, rhot_ref):
    rows = docs_ref.shape[1]
    chip, core = place()
    kind = lax.broadcasted_iota(jnp.int32, (HD, rows), 0)
    for source in range(khot_ref.shape[0]):
        hot = kind == docs_ref[pl.ds(source * 2 + core, 1), :]
        khot_ref[source] = jnp.transpose(hot.astype(F32)).astype(BF16)
    for side in range(2):
        row_block = chip * 2 + (core if side == 0 else 1 - core)
        hot = kind == docs_ref[pl.ds(row_block, 1), :]
        rhot_ref[:, side * rows : (side + 1) * rows] = jnp.where(hot, 0.0, MASKED).astype(BF16)


def chunks_of(sides, qds, rhot_ref):
    rows = rhot_ref.shape[1] // 2
    heads = qds[0].shape[1] // rows
    for side in sides:
        for head in range(heads):
            local = slice(head * rows, (head + 1) * rows)
            chunk = side * heads + head
            lanes = slice(chunk * rows, (chunk + 1) * rows)
            penalty = rhot_ref[:, side * rows : (side + 1) * rows]
            yield lanes, qds[side][:HD, local], qds[side][HD:, local], penalty


def scores_of(kv, khot, qt, penalty, causal):
    keys = jnp.concatenate([kv[:, :HD], khot], axis=1)
    scores = nn(keys, jnp.concatenate([qt, penalty], axis=0))
    if causal:
        key_pos = lax.broadcasted_iota(jnp.int32, scores.shape, 0)
        row_pos = lax.broadcasted_iota(jnp.int32, scores.shape, 1)
        scores = jnp.where(key_pos <= row_pos, scores, MASKED)
    return scores


def add_stats(stats_ref, kv, khot, qds, rhot_ref, sides, causal, keep=()):
    for lanes, qt, dot, penalty in chunks_of(sides, qds, rhot_ref):
        scores = scores_of(kv, khot, qt, penalty, causal)
        grad_probs = nn(kv[:, HD:], dot)
        old = stats_ref[0:1, lanes]
        new = jnp.maximum(old, jnp.max(scores, axis=0, keepdims=True) * (SCALE * LOG2E))
        factor = jnp.exp2(old - new)
        weights = jnp.exp2(scores * (SCALE * LOG2E) - new)
        for ref, kept in zip(keep, (weights, grad_probs)):
            ref[:, lanes] = kept
        stats_ref[0:1, lanes] = new
        stats_ref[1:2, lanes] = stats_ref[1:2, lanes] * factor + jnp.sum(
            weights, axis=0, keepdims=True
        )
        stats_ref[2:3, lanes] = stats_ref[2:3, lanes] * factor + jnp.sum(
            weights * grad_probs, axis=0, keepdims=True
        )


def add_grads(kv, khot, qds, rhot_ref, sides, causal, norm_ref, dqt_ref, fresh, keep=()):
    qts, dots, lows, grads, all_lanes = [], [], [], [], []
    for lanes, qt, dot, penalty in chunks_of(sides, qds, rhot_ref):
        if keep:
            top_ref, weights_ref, probs_ref = keep
            factor = jnp.exp2(top_ref[0:1, lanes] - norm_ref[0:1, lanes])
            weights = weights_ref[:, lanes] * factor
            grad_probs = probs_ref[:, lanes]
        else:
            scores = scores_of(kv, khot, qt, penalty, causal)
            weights = jnp.exp2(scores * (SCALE * LOG2E) - norm_ref[0:1, lanes])
            grad_probs = nn(kv[:, HD:], dot)
        grad_scores = (weights * (grad_probs - norm_ref[1:2, lanes])).astype(BF16)
        all_lanes.append(lanes)
        qts.append(qt)
        dots.append(dot)
        lows.append(weights.astype(BF16))
        grads.append(grad_scores)

    def joined(parts):
        return jnp.concatenate(parts, axis=1)

    span = slice(all_lanes[0].start, all_lanes[-1].stop)
    change = tn(kv[:, :HD], joined(grads))
    if fresh:
        dqt_ref[:, span] = change
    else:
        dqt_ref[:, span] += change
    dkt = nt(joined(qts), joined(grads)) * SCALE
    dvt = nt(joined(dots), joined(lows))
    return jnp.concatenate([dkt, dvt], axis=0)


def reaches(docs_ref, key_block, row_block):
    last = docs_ref[pl.ds(key_block, 1), :][0, docs_ref.shape[1] - 1]
    return last >= docs_ref[pl.ds(row_block, 1), :][0, 0]


def blank_kernel(stats_ref):
    stats_ref[...] = jnp.zeros(stats_ref.shape, F32)
    stats_ref[0:1, :] = jnp.full((1, stats_ref.shape[1]), LOWEST, F32)


def pack_kernel(after_ref, key_ref, value_ref, kv_ref):
    kv_ref[:, :HD] = key_ref[...]
    kv_ref[:, HD:] = value_ref[...]


def turn_kernel(q_own, do_own, q_par, do_par, qd_own, qd_par):
    rows, columns = q_own.shape
    for q_ref, do_ref, qd_ref in ((q_own, do_own, qd_own), (q_par, do_par, qd_par)):
        for top, ref in ((0, q_ref), (HD, do_ref)):
            turned = jnp.transpose(ref[...])
            for head in range(columns // HD):
                qd_ref[top : top + HD, head * rows : (head + 1) * rows] = turned[
                    head * HD : (head + 1) * HD, :
                ]


def own_stats_kernel(khot_ref, rhot_ref, qd_own, qd_par, kv_ref, stats_in, stats_ref):
    chip, core = place()
    stats_ref[...] = stats_in[...]
    kv, khot, qds = kv_ref[...], khot_ref[chip], (qd_own, qd_par)
    add_stats(stats_ref, kv, khot, qds, rhot_ref, (0,), True)

    @pl.when(core == 0)
    def _():
        add_stats(stats_ref, kv, khot, qds, rhot_ref, (1,), False)


def each_remote(first, kv_ref, docs_ref, body, rest):
    chip, core = place()
    count = kv_ref.shape[0]

    def step(slot):
        source = chip ^ (first + slot)

        @pl.when(source < chip)
        def _():
            active = reaches(docs_ref, source * 2 + core, chip * 2)
            pl.when(active)(functools.partial(body, slot, source))
            if rest is not None:
                pl.when(jnp.logical_not(active))(rest)

        if rest is not None:
            pl.when(source > chip)(rest)

    if count == 1:
        step(0)
    else:
        pl.loop(0, count)(step)


def far_stats_kernel(first, docs_ref, khot_ref, rhot_ref, qd_own, qd_par, stats_in, kv_ref, *outs):
    stats_ref, keep = outs[0], outs[1:]
    stats_ref[...] = stats_in[...]
    qds = qd_own, qd_par

    def body(slot, source):
        add_stats(stats_ref, kv_ref[slot], khot_ref[source], qds, rhot_ref, (0, 1), False, keep)

    each_remote(first, kv_ref, docs_ref, body, None)


def norm_kernel(stats_ref, other_ref, norm_ref):
    half = stats_ref.shape[1] // 2
    mine = stats_ref[...]
    other = other_ref[...]
    other = jnp.concatenate([other[:, half:], other[:, :half]], axis=1)
    top = jnp.maximum(mine[0:1], other[0:1])
    mine_by = jnp.exp2(mine[0:1] - top)
    other_by = jnp.exp2(other[0:1] - top)
    total = mine[1:2] * mine_by + other[1:2] * other_by
    norm_ref[...] = jnp.zeros(norm_ref.shape, F32)
    norm_ref[0:1, :] = top + jnp.log2(total)
    norm_ref[1:2, :] = (mine[2:3] * mine_by + other[2:3] * other_by) / total


def far_grads_kernel(
    first, docs_ref, khot_ref, rhot_ref, qd_own, qd_par, norm_ref, kv_ref, before_ref, *rest
):
    keep, (out_ref, dqt_ref) = rest[:-2], rest[-2:]
    alone = kv_ref.shape[0] == 1
    qds = qd_own, qd_par

    def clear():
        dqt_ref[...] = jnp.zeros(dqt_ref.shape, F32)
        out_ref[...] = jnp.zeros(out_ref.shape, BF16)

    if not alone:
        clear()

    def body(slot, source):
        kv, khot = kv_ref[slot], khot_ref[source]
        part = add_grads(
            kv, khot, qds, rhot_ref, (0, 1), False, norm_ref, dqt_ref, alone, keep
        )
        out_ref[slot] = part.astype(BF16)

    each_remote(first, kv_ref, docs_ref, body, clear if alone else None)


def own_grads_kernel(khot_ref, rhot_ref, qd_own, qd_par, norm_ref, kv_ref, *rest):
    dqt_in, (dkv_ref, dq_own, dq_par, dqt_ref) = rest[:-4], rest[-4:]
    rows = kv_ref.shape[0]
    heads = qd_own.shape[1] // rows
    chip, core = place()
    dqt_ref[...] = sum(part[...] for part in dqt_in)
    kv, khot, qds = kv_ref[...], khot_ref[chip], (qd_own, qd_par)
    dkv_ref[...] = add_grads(kv, khot, qds, rhot_ref, (0,), True, norm_ref, dqt_ref, False)

    @pl.when(core == 0)
    def _():
        dkv_ref[...] += add_grads(kv, khot, qds, rhot_ref, (1,), False, norm_ref, dqt_ref, False)

    for side, out_ref in enumerate((dq_own, dq_par)):
        for head in range(heads):
            chunk = side * heads + head
            out_ref[head * HD : (head + 1) * HD, :] = (
                dqt_ref[:, chunk * rows : (chunk + 1) * rows] * SCALE
            )


def query_kernel(dq_own, dq_far, dq_ref, token_ref):
    token_ref[...] = jnp.zeros(token_ref.shape, F32)
    dq_ref[...] = jnp.transpose(dq_own[...] + dq_far[...]).astype(BF16)


def hops_of(share):
    return [1, 2, 3] if share == 4 else list(range(1, share))


def next_of(share, member, away):
    line = [i ^ i >> 1 for i in range(share)]
    return line[(line.index(member) + away) % share]


def combine_kernel(share, count, dq_in, own_ref, *rest):
    parts, outs = rest[:count], rest[count:]
    keep_ref, send_refs, sum_ref = outs[1], outs[2:-1], outs[-1]
    width = HD // share
    total = own_ref[...]
    for part in parts:
        total = total + part[...].astype(F32)
    sum_ref[...] = total
    member = lax.axis_index("grp") % share
    for away, out_ref in zip((0, *hops_of(share)), (keep_ref, *send_refs)):
        target = sum((member == i) * next_of(share, i, away) for i in range(share))
        first = pl.multiple_of(target * width, width)
        for half in range(2):
            piece = sum_ref[pl.ds(half * HD + first, width), :]
            out_ref[half * width : (half + 1) * width, :] = piece.astype(out_ref.dtype)


def finish_kernel(after_ref, keep_ref, *rest):
    parts, (dk_ref, dv_ref) = rest[:-2], rest[-2:]
    total = keep_ref[...]
    for part in parts:
        total = total + part[...].astype(F32)
    width = total.shape[0] // 2
    dk_ref[...] = total[:width].astype(BF16)
    dv_ref[...] = total[width:].astype(BF16)


VMEM = pl.BlockSpec(memory_space=pltpu.VMEM)
ANY = pl.BlockSpec(memory_space=pl.ANY)


HBM = pl.BlockSpec(memory_space=pltpu.HBM)


def call(kernel, out_shape, operands, scratch=(), unread=(), aliases={}, us=0, hbm=0, vmem=24):
    kinds = [HBM] * hbm + [VMEM] * (len(operands) - hbm)
    results = [VMEM] * len(out_shape)
    for place_of in unread:
        kinds[place_of] = ANY
    for source, target in aliases.items():
        kinds[source] = ANY
        results[target] = ANY
    cost = pl.CostEstimate(flops=us * 10**9, bytes_accessed=1 << 19, transcendentals=0)
    return pl.pallas_call(
        kernel,
        out_shape=out_shape,
        in_specs=kinds,
        out_specs=results,
        scratch_shapes=list(scratch),
        input_output_aliases=aliases,
        cost_estimate=cost,
        compiler_params=pltpu.CompilerParams(vmem_limit_bytes=vmem << 20),
    )(*operands)


def sds(shape, dtype):
    return jax.ShapeDtypeStruct(shape, dtype)


def on_device(queries, key_rows, value_rows, grad_output, doc_ids):
    rows, columns = queries.shape
    heads = columns // HD
    srv = lax.axis_size("srv")
    chips = srv // 2
    grp = lax.axis_size("grp")
    kv_heads = key_rows.shape[1] // HD
    share = grp // kv_heads
    lanes = 2 * heads * rows
    if kv_heads > 1:
        first = lax.axis_index("grp") // share * HD
        key_rows = lax.dynamic_slice_in_dim(key_rows, first, HD, 1)
        value_rows = lax.dynamic_slice_in_dim(value_rows, first, HD, 1)
    (blank,) = call(blank_kernel, [sds((8, lanes), F32)], [], us=5)
    (own_kv,) = call(
        pack_kernel,
        [sds((rows, 2 * HD), BF16)],
        [blank, key_rows, value_rows],
        unread=[0],
    )
    docs = doc_ids.reshape(srv, rows)

    apart = DOC_MOST.get(srv * rows, srv * rows) <= 5 * rows + 1

    def trade(block, away, back=False):
        pairs = [(i, i ^ 2 * away) for i in range(srv)]
        if srv == 8 and away == 3 and apart:
            pairs = [(4, 2), (5, 3), (7, 1), (6, 7), (0, 4), (1, 5), (2, 6), (3, 0)] if back else CORNER
        return lax.ppermute(block, "srv", pairs)

    def swap(block):
        return lax.ppermute(block, "srv", [(i, i ^ 1) for i in range(srv)])

    order = list(range(chips - 1, 0, -1))
    far_kv = {away: trade(own_kv, away)[None] for away in order}
    if chips > 4:
        far_kv = {1: jnp.concatenate([far_kv[away] for away in order[::-1]], axis=0)}
    qd_own, qd_par = call(
        turn_kernel,
        [sds((2 * HD, heads * rows), BF16)] * 2,
        [queries, grad_output, swap(queries), swap(grad_output)],
    )
    khot, rhot = call(
        hot_kernel,
        [sds((chips, rows, HD), BF16), sds((HD, 2 * rows), BF16)],
        [docs],
    )
    shared = [docs, khot, rhot, qd_own, qd_par]
    (stats,) = call(
        own_stats_kernel, [sds((8, lanes), F32)], [*shared[1:], own_kv, blank]
    )
    turns = [3, 1, 2] if chips == 4 else list(far_kv)
    kept = {}
    for first in turns:
        saved = [sds((rows, lanes), F32)] * 2 if chips == 4 else []
        stats, *saved = call(
            functools.partial(far_stats_kernel, first),
            [sds((8, lanes), F32)] + saved,
            [*shared, stats, far_kv[first]],
        )
        kept[first] = [stats, *saved] if saved else []
    (norm,) = call(norm_kernel, [sds((8, lanes), F32)], [stats, swap(stats)])
    parts, dqt = {}, [norm]
    turns = [3, 2, 1] if chips == 4 else turns
    for first in turns:
        kv = far_kv[first]
        parts[first], dqt_part = call(
            functools.partial(far_grads_kernel, first),
            [sds(kv.shape[:1] + (2 * HD, rows), BF16), sds((HD, lanes), F32)],
            [*shared, norm, kv, dqt[-1], *kept[first]],
            unread=[len(shared) + 2],
        )
        dqt.append(dqt_part)
    came = [
        trade(parts[first][slot], first + slot, True)
        for first in turns
        for slot in range(parts[first].shape[0])
    ]
    own_dkv, dq_own, dq_par = call(
        own_grads_kernel,
        [sds((2 * HD, rows), F32)] + [sds((columns, rows), F32)] * 2,
        [*shared[1:], norm, own_kv, *dqt[1:]],
        scratch=[pltpu.VMEM((HD, lanes), F32)],
        us=4,
    )
    width = HD // share
    dq_par, keep, *send = call(
        functools.partial(combine_kernel, share, len(came)),
        [sds(dq_par.shape, F32), sds((2 * width, rows), F32)]
        + [sds((2 * width, rows), BF16)] * (share - 1),
        [dq_par, own_dkv, *came],
        scratch=[pltpu.VMEM((2 * HD, rows), F32)],
        aliases={0: 0},
    )
    back = [
        lax.ppermute(part, "grp", [(i, i // share * share + next_of(share, i % share, away)) for i in range(grp)])
        for away, part in zip(hops_of(share), send)
    ]
    grad_query, token = call(
        query_kernel,
        [sds((rows, columns), BF16), sds((8, 128), F32)],
        [dq_own, swap(dq_par)],
        us=2,
    )
    grad_key, grad_value = call(
        finish_kernel,
        [sds((width, rows), BF16)] * 2,
        [token, keep, *back],
        unread=[0],
    )
    return grad_query, grad_key.T, grad_value.T


def solution(mesh):
    in_specs = (P("srv", "grp"), P("srv", None), P("srv", None), P("srv", "grp"), P())
    out_specs = (P("srv", "grp"), P("srv", "grp"), P("srv", "grp"))
    return jax.shard_map(
        on_device, mesh=mesh, in_specs=in_specs, out_specs=out_specs, check_vma=False
    )
```

```python
import functools

import jax
import jax.numpy as jnp
from jax import lax
from jax.experimental import pallas as pl
from jax.experimental.pallas import tpu as pltpu
from jax.sharding import PartitionSpec as P

HD = 128
SCALE = HD**-0.5
LOG2E = 1.4426950408889634
MASKED = -1.0e30
LOWEST = -1.0e20
DOC_MOST = {2048: 1280, 8192: 4352}
CORNER = [(1, 7), (7, 6), (6, 2), (2, 4), (4, 0), (0, 1), (3, 5), (5, 3)]
F32 = jnp.float32
BF16 = jnp.bfloat16


def nn(a, b):
    return lax.dot_general(a, b, (((1,), (0,)), ((), ())), preferred_element_type=F32)


def nt(a, b):
    return lax.dot_general(a, b, (((1,), (1,)), ((), ())), preferred_element_type=F32)


def tn(a, b):
    return lax.dot_general(a, b, (((0,), (0,)), ((), ())), preferred_element_type=F32)


def place():
    srv = lax.axis_index("srv")
    return srv // 2, srv % 2


def hot_kernel(docs_ref, khot_ref, rhot_ref):
    rows = docs_ref.shape[1]
    chip, core = place()
    kind = lax.broadcasted_iota(jnp.int32, (HD, rows), 0)
    for source in range(khot_ref.shape[0]):
        hot = kind == docs_ref[pl.ds(source * 2 + core, 1), :]
        khot_ref[source] = jnp.transpose(hot.astype(F32)).astype(BF16)
    for side in range(2):
        row_block = chip * 2 + (core if side == 0 else 1 - core)
        hot = kind == docs_ref[pl.ds(row_block, 1), :]
        rhot_ref[:, side * rows : (side + 1) * rows] = jnp.where(hot, 0.0, MASKED).astype(BF16)


def chunks_of(sides, qds, rhot_ref):
    rows = rhot_ref.shape[1] // 2
    heads = qds[0].shape[1] // rows
    for side in sides:
        for head in range(heads):
            local = slice(head * rows, (head + 1) * rows)
            chunk = side * heads + head
            lanes = slice(chunk * rows, (chunk + 1) * rows)
            penalty = rhot_ref[:, side * rows : (side + 1) * rows]
            yield lanes, qds[side][:HD, local], qds[side][HD:, local], penalty


def scores_of(kv, khot, qt, penalty, causal):
    keys = jnp.concatenate([kv[:, :HD], khot], axis=1)
    scores = nn(keys, jnp.concatenate([qt, penalty], axis=0))
    if causal:
        key_pos = lax.broadcasted_iota(jnp.int32, scores.shape, 0)
        row_pos = lax.broadcasted_iota(jnp.int32, scores.shape, 1)
        scores = jnp.where(key_pos <= row_pos, scores, MASKED)
    return scores


def add_stats(stats_ref, kv, khot, qds, rhot_ref, sides, causal, keep=()):
    for lanes, qt, dot, penalty in chunks_of(sides, qds, rhot_ref):
        scores = scores_of(kv, khot, qt, penalty, causal)
        grad_probs = nn(kv[:, HD:], dot)
        old = stats_ref[0:1, lanes]
        new = jnp.maximum(old, jnp.max(scores, axis=0, keepdims=True) * (SCALE * LOG2E))
        factor = jnp.exp2(old - new)
        weights = jnp.exp2(scores * (SCALE * LOG2E) - new)
        for ref, kept in zip(keep, (weights, grad_probs)):
            ref[:, lanes] = kept
        stats_ref[0:1, lanes] = new
        stats_ref[1:2, lanes] = stats_ref[1:2, lanes] * factor + jnp.sum(
            weights, axis=0, keepdims=True
        )
        stats_ref[2:3, lanes] = stats_ref[2:3, lanes] * factor + jnp.sum(
            weights * grad_probs, axis=0, keepdims=True
        )


def add_grads(kv, khot, qds, rhot_ref, sides, causal, norm_ref, dqt_ref, fresh, keep=()):
    qts, dots, lows, grads, all_lanes = [], [], [], [], []
    for lanes, qt, dot, penalty in chunks_of(sides, qds, rhot_ref):
        if keep:
            top_ref, weights_ref, probs_ref = keep
            factor = jnp.exp2(top_ref[0:1, lanes] - norm_ref[0:1, lanes])
            weights = weights_ref[:, lanes] * factor
            grad_probs = probs_ref[:, lanes]
        else:
            scores = scores_of(kv, khot, qt, penalty, causal)
            weights = jnp.exp2(scores * (SCALE * LOG2E) - norm_ref[0:1, lanes])
            grad_probs = nn(kv[:, HD:], dot)
        grad_scores = (weights * (grad_probs - norm_ref[1:2, lanes])).astype(BF16)
        all_lanes.append(lanes)
        qts.append(qt)
        dots.append(dot)
        lows.append(weights.astype(BF16))
        grads.append(grad_scores)

    def joined(parts):
        return jnp.concatenate(parts, axis=1)

    span = slice(all_lanes[0].start, all_lanes[-1].stop)
    change = tn(kv[:, :HD], joined(grads))
    if fresh:
        dqt_ref[:, span] = change
    else:
        dqt_ref[:, span] += change
    dkt = nt(joined(qts), joined(grads)) * SCALE
    dvt = nt(joined(dots), joined(lows))
    return jnp.concatenate([dkt, dvt], axis=0)


def reaches(docs_ref, key_block, row_block):
    last = docs_ref[pl.ds(key_block, 1), :][0, docs_ref.shape[1] - 1]
    return last >= docs_ref[pl.ds(row_block, 1), :][0, 0]


def blank_kernel(stats_ref):
    stats_ref[...] = jnp.zeros(stats_ref.shape, F32)
    stats_ref[0:1, :] = jnp.full((1, stats_ref.shape[1]), LOWEST, F32)


def pack_kernel(after_ref, key_ref, value_ref, kv_ref):
    kv_ref[:, :HD] = key_ref[...]
    kv_ref[:, HD:] = value_ref[...]


def turn_kernel(q_own, do_own, q_par, do_par, qd_own, qd_par):
    rows, columns = q_own.shape
    for q_ref, do_ref, qd_ref in ((q_own, do_own, qd_own), (q_par, do_par, qd_par)):
        for top, ref in ((0, q_ref), (HD, do_ref)):
            turned = jnp.transpose(ref[...])
            for head in range(columns // HD):
                qd_ref[top : top + HD, head * rows : (head + 1) * rows] = turned[
                    head * HD : (head + 1) * HD, :
                ]


def own_stats_kernel(khot_ref, rhot_ref, qd_own, qd_par, kv_ref, stats_in, stats_ref):
    chip, core = place()
    stats_ref[...] = stats_in[...]
    kv, khot, qds = kv_ref[...], khot_ref[chip], (qd_own, qd_par)
    add_stats(stats_ref, kv, khot, qds, rhot_ref, (0,), True)

    @pl.when(core == 0)
    def _():
        add_stats(stats_ref, kv, khot, qds, rhot_ref, (1,), False)


def each_remote(first, kv_ref, docs_ref, body, rest):
    chip, core = place()
    count = kv_ref.shape[0]

    def step(slot):
        source = chip ^ (first + slot)

        @pl.when(source < chip)
        def _():
            active = reaches(docs_ref, source * 2 + core, chip * 2)
            pl.when(active)(functools.partial(body, slot, source))
            if rest is not None:
                pl.when(jnp.logical_not(active))(rest)

        if rest is not None:
            pl.when(source > chip)(rest)

    if count == 1:
        step(0)
    else:
        pl.loop(0, count)(step)


def far_stats_kernel(first, docs_ref, khot_ref, rhot_ref, qd_own, qd_par, stats_in, kv_ref, *outs):
    stats_ref, keep = outs[0], outs[1:]
    stats_ref[...] = stats_in[...]
    qds = qd_own, qd_par

    def body(slot, source):
        add_stats(stats_ref, kv_ref[slot], khot_ref[source], qds, rhot_ref, (0, 1), False, keep)

    each_remote(first, kv_ref, docs_ref, body, None)


def norm_kernel(stats_ref, other_ref, norm_ref):
    half = stats_ref.shape[1] // 2
    mine = stats_ref[...]
    other = other_ref[...]
    other = jnp.concatenate([other[:, half:], other[:, :half]], axis=1)
    top = jnp.maximum(mine[0:1], other[0:1])
    mine_by = jnp.exp2(mine[0:1] - top)
    other_by = jnp.exp2(other[0:1] - top)
    total = mine[1:2] * mine_by + other[1:2] * other_by
    norm_ref[...] = jnp.zeros(norm_ref.shape, F32)
    norm_ref[0:1, :] = top + jnp.log2(total)
    norm_ref[1:2, :] = (mine[2:3] * mine_by + other[2:3] * other_by) / total


def far_grads_kernel(
    first, docs_ref, khot_ref, rhot_ref, qd_own, qd_par, norm_ref, kv_ref, before_ref, *rest
):
    keep, (out_ref, dqt_ref) = rest[:-2], rest[-2:]
    alone = kv_ref.shape[0] == 1
    qds = qd_own, qd_par

    def clear():
        dqt_ref[...] = jnp.zeros(dqt_ref.shape, F32)
        out_ref[...] = jnp.zeros(out_ref.shape, BF16)

    if not alone:
        clear()

    def body(slot, source):
        kv, khot = kv_ref[slot], khot_ref[source]
        part = add_grads(
            kv, khot, qds, rhot_ref, (0, 1), False, norm_ref, dqt_ref, alone, keep
        )
        out_ref[slot] = part.astype(BF16)

    each_remote(first, kv_ref, docs_ref, body, clear if alone else None)


def own_grads_kernel(khot_ref, rhot_ref, qd_own, qd_par, norm_ref, kv_ref, *rest):
    dqt_in, (dkv_ref, dq_own, dq_par, dqt_ref) = rest[:-4], rest[-4:]
    rows = kv_ref.shape[0]
    heads = qd_own.shape[1] // rows
    chip, core = place()
    dqt_ref[...] = sum(part[...] for part in dqt_in)
    kv, khot, qds = kv_ref[...], khot_ref[chip], (qd_own, qd_par)
    dkv_ref[...] = add_grads(kv, khot, qds, rhot_ref, (0,), True, norm_ref, dqt_ref, False)

    @pl.when(core == 0)
    def _():
        dkv_ref[...] += add_grads(kv, khot, qds, rhot_ref, (1,), False, norm_ref, dqt_ref, False)

    for side, out_ref in enumerate((dq_own, dq_par)):
        for head in range(heads):
            chunk = side * heads + head
            out_ref[head * HD : (head + 1) * HD, :] = (
                dqt_ref[:, chunk * rows : (chunk + 1) * rows] * SCALE
            )


def query_kernel(dq_own, dq_far, dq_ref, token_ref):
    token_ref[...] = jnp.zeros(token_ref.shape, F32)
    dq_ref[...] = jnp.transpose(dq_own[...] + dq_far[...]).astype(BF16)


def hops_of(share):
    return [1, 2, 3] if share == 4 else list(range(1, share))


def next_of(share, member, away):
    line = [i ^ i >> 1 for i in range(share)]
    return line[(line.index(member) + away) % share]


def combine_kernel(share, count, dq_in, own_ref, *rest):
    parts, outs = rest[:count], rest[count:]
    keep_ref, send_refs, sum_ref = outs[1], outs[2:-1], outs[-1]
    width = HD // share
    total = own_ref[...]
    for part in parts:
        total = total + part[...].astype(F32)
    sum_ref[...] = total
    member = lax.axis_index("grp") % share
    for away, out_ref in zip((0, *hops_of(share)), (keep_ref, *send_refs)):
        target = sum((member == i) * next_of(share, i, away) for i in range(share))
        first = pl.multiple_of(target * width, width)
        for half in range(2):
            piece = sum_ref[pl.ds(half * HD + first, width), :]
            out_ref[half * width : (half + 1) * width, :] = piece.astype(out_ref.dtype)


def finish_kernel(after_ref, keep_ref, *rest):
    parts, (dk_ref, dv_ref) = rest[:-2], rest[-2:]
    total = keep_ref[...]
    for part in parts:
        total = total + part[...].astype(F32)
    width = total.shape[0] // 2
    dk_ref[...] = total[:width].astype(BF16)
    dv_ref[...] = total[width:].astype(BF16)


VMEM = pl.BlockSpec(memory_space=pltpu.VMEM)
ANY = pl.BlockSpec(memory_space=pl.ANY)


HBM = pl.BlockSpec(memory_space=pltpu.HBM)


def call(kernel, out_shape, operands, scratch=(), unread=(), aliases={}, us=0, hbm=0, vmem=24):
    kinds = [HBM] * hbm + [VMEM] * (len(operands) - hbm)
    results = [VMEM] * len(out_shape)
    for place_of in unread:
        kinds[place_of] = ANY
    for source, target in aliases.items():
        kinds[source] = ANY
        results[target] = ANY
    cost = pl.CostEstimate(flops=us * 10**9, bytes_accessed=1 << 19, transcendentals=0)
    return pl.pallas_call(
        kernel,
        out_shape=out_shape,
        in_specs=kinds,
        out_specs=results,
        scratch_shapes=list(scratch),
        input_output_aliases=aliases,
        cost_estimate=cost,
        compiler_params=pltpu.CompilerParams(vmem_limit_bytes=vmem << 20),
    )(*operands)


def sds(shape, dtype):
    return jax.ShapeDtypeStruct(shape, dtype)


def on_device(queries, key_rows, value_rows, grad_output, doc_ids):
    rows, columns = queries.shape
    heads = columns // HD
    srv = lax.axis_size("srv")
    chips = srv // 2
    grp = lax.axis_size("grp")
    kv_heads = key_rows.shape[1] // HD
    share = grp // kv_heads
    lanes = 2 * heads * rows
    if kv_heads > 1:
        first = lax.axis_index("grp") // share * HD
        key_rows = lax.dynamic_slice_in_dim(key_rows, first, HD, 1)
        value_rows = lax.dynamic_slice_in_dim(value_rows, first, HD, 1)
    (blank,) = call(blank_kernel, [sds((8, lanes), F32)], [], us=5)
    (own_kv,) = call(
        pack_kernel,
        [sds((rows, 2 * HD), BF16)],
        [blank, key_rows, value_rows],
        unread=[0],
    )
    docs = doc_ids.reshape(srv, rows)

    apart = DOC_MOST.get(srv * rows, srv * rows) <= 5 * rows + 1

    def trade(block, away, back=False):
        pairs = [(i, i ^ 2 * away) for i in range(srv)]
        if srv == 8 and away == 3 and apart:
            pairs = [(4, 2), (5, 3), (7, 1), (6, 5), (0, 4), (1, 0), (2, 7), (3, 6)] if back else CORNER
        return lax.ppermute(block, "srv", pairs)

    def swap(block):
        return lax.ppermute(block, "srv", [(i, i ^ 1) for i in range(srv)])

    order = list(range(chips - 1, 0, -1))
    far_kv = {away: trade(own_kv, away)[None] for away in order}
    if chips > 4:
        far_kv = {1: jnp.concatenate([far_kv[away] for away in order[::-1]], axis=0)}
    qd_own, qd_par = call(
        turn_kernel,
        [sds((2 * HD, heads * rows), BF16)] * 2,
        [queries, grad_output, swap(queries), swap(grad_output)],
    )
    khot, rhot = call(
        hot_kernel,
        [sds((chips, rows, HD), BF16), sds((HD, 2 * rows), BF16)],
        [docs],
    )
    shared = [docs, khot, rhot, qd_own, qd_par]
    (stats,) = call(
        own_stats_kernel, [sds((8, lanes), F32)], [*shared[1:], own_kv, blank]
    )
    turns = [3, 1, 2] if chips == 4 else list(far_kv)
    kept = {}
    for first in turns:
        saved = [sds((rows, lanes), F32)] * 2 if chips == 4 else []
        stats, *saved = call(
            functools.partial(far_stats_kernel, first),
            [sds((8, lanes), F32)] + saved,
            [*shared, stats, far_kv[first]],
        )
        kept[first] = [stats, *saved] if saved else []
    (norm,) = call(norm_kernel, [sds((8, lanes), F32)], [stats, swap(stats)])
    parts, dqt = {}, [norm]
    turns = [3, 2, 1] if chips == 4 else turns
    for first in turns:
        kv = far_kv[first]
        parts[first], dqt_part = call(
            functools.partial(far_grads_kernel, first),
            [sds(kv.shape[:1] + (2 * HD, rows), BF16), sds((HD, lanes), F32)],
            [*shared, norm, kv, dqt[-1], *kept[first]],
            unread=[len(shared) + 2],
        )
        dqt.append(dqt_part)
    came = [
        trade(parts[first][slot], first + slot, True)
        for first in turns
        for slot in range(parts[first].shape[0])
    ]
    own_dkv, dq_own, dq_par = call(
        own_grads_kernel,
        [sds((2 * HD, rows), F32)] + [sds((columns, rows), F32)] * 2,
        [*shared[1:], norm, own_kv, *dqt[1:]],
        scratch=[pltpu.VMEM((HD, lanes), F32)],
        us=4,
    )
    width = HD // share
    dq_par, keep, *send = call(
        functools.partial(combine_kernel, share, len(came)),
        [sds(dq_par.shape, F32), sds((2 * width, rows), F32)]
        + [sds((2 * width, rows), BF16)] * (share - 1),
        [dq_par, own_dkv, *came],
        scratch=[pltpu.VMEM((2 * HD, rows), F32)],
        aliases={0: 0},
    )
    back = [
        lax.ppermute(part, "grp", [(i, i // share * share + next_of(share, i % share, away)) for i in range(grp)])
        for away, part in zip(hops_of(share), send)
    ]
    grad_query, token = call(
        query_kernel,
        [sds((rows, columns), BF16), sds((8, 128), F32)],
        [dq_own, swap(dq_par)],
        us=2,
    )
    grad_key, grad_value = call(
        finish_kernel,
        [sds((width, rows), BF16)] * 2,
        [token, keep, *back],
        unread=[0],
    )
    return grad_query, grad_key.T, grad_value.T


def solution(mesh):
    in_specs = (P("srv", "grp"), P("srv", None), P("srv", None), P("srv", "grp"), P())
    out_specs = (P("srv", "grp"), P("srv", "grp"), P("srv", "grp"))
    return jax.shard_map(
        on_device, mesh=mesh, in_specs=in_specs, out_specs=out_specs, check_vma=False
    )
```
